512 devices in a mesh: dp: 16 (over z_hi, x), space: 32 (over z_lo, y, core).
Axes of the slice: x: 4, y: 8, z: 8 (z_hi: 4, z_lo: 2; z = z_hi * 2 + z_lo), core: 2. Of those that a mesh axis runs over, the one named last changes fastest.
Arguments:
- activations: bfloat16 [16, 64, 14, 14, 256], P('dp', 'space'), may hold values from -7 to 7
- tissue: int32 [16, 64, 14, 14], P('dp', 'space'), may hold values from 0 to 1, as said below
- neighbours: int32 [16, 64, 8], P('dp', 'space'), may hold values from -1 to 63, as said below
- w_reduce: bfloat16 [256, 256], replicated, may hold values from -0.375 to 0.375
- w_group: bfloat16 [3, 3, 8, 256], replicated, may hold values from -0.75 to 0.75
- norm_gain: float32 [256], replicated, may hold values from 0.25 to 1.75
- norm_bias: float32 [256], replicated, may hold values from -3 to 3
- w_expand: bfloat16 [256, 512], replicated, may hold values from -0.375 to 0.375
- cotangent: bfloat16 [16, 64, 14, 14, 512], P('dp', 'space'), may hold values from -7 to 7
Outputs:
- input_grad: bfloat16 [16, 64, 14, 14, 256], P('dp', 'space')
- reduce_grad: float32 [256, 256], replicated
- group_grad: float32 [3, 3, 8, 256], replicated
- gain_grad: float32 [256], replicated
- bias_grad: float32 [256], replicated
- expand_grad: float32 [256, 512], replicated
The draws below stay inside these ranges and needn't reach their ends.
Inputs may be any that keep to these rules, and one draw needn't show every extreme that they name: `neighbours`: tile slot t of a slide lies at row t // 4 and column t % 4 of its grid; an entry names the slot at the stated side only if both tiles hold tissue, so that tile b is a neighbour of tile a at one side exactly when a is the neighbour of b at the opposite side. Slots 0, 62 and 63 hold tissue. `tissue`: slots absent from a slide are 0 throughout; a present tile is 1 on the pixels its draw marks, always including its first pixel.
All inputs are finite; a program needn't handle non-finite values.
Results may differ from the reference program's by a relative error of at most 0.011.
Values may be sent and summed in bfloat16 or wider, within the bound.
No kernel may reach another device: no remote copies, remote signals or barrier semaphores. Data moves between devices by JAX's collectives and lax.ppermute only.
A program may use at most 128 MiB of HBM per device.

```python
import jax
import jax.numpy as jnp
from jax import lax

CH = 256
OUT_CH = 512
GROUP_WIDTH = 8
TILE_SIDE = 14
GRID_WIDE = 4
TILES = 64
SLIDES = 16


def present_tiles(key):
    keep = jax.random.randint(jax.random.fold_in(key, 11), (SLIDES, TILES), 0, 5) > 0
    slots = jnp.arange(TILES)
    forced = (slots == 0) | (slots >= TILES - 2)
    return keep | forced[None, :]


def draw_tissue(key, part):
    present = present_tiles(key)
    key = jax.random.fold_in(key, 3)
    pixels = jax.random.randint(key, (SLIDES, TILES, TILE_SIDE, TILE_SIDE), 0, 4) > 0
    first = (jnp.arange(TILE_SIDE)[:, None] == 0) & (jnp.arange(TILE_SIDE)[None, :] == 0)
    return (present[:, :, None, None] & (pixels | first[None, None])).astype(jnp.int32)


def draw_neighbours(key, part):
    present = present_tiles(key)
    slots = jnp.arange(TILES)
    grid_row = slots // GRID_WIDE
    grid_col = slots % GRID_WIDE
    grid_rows = TILES // GRID_WIDE
    steps_list = [(-1, 0), (1, 0), (0, -1), (0, 1), (-1, -1), (-1, 1), (1, -1), (1, 1)]
    columns = []
    for row_step, col_step in steps_list:
        new_row = grid_row + row_step
        new_col = grid_col + col_step
        inside = (new_row >= 0) & (new_row < grid_rows) & (new_col >= 0) & (new_col < GRID_WIDE)
        target = jnp.clip(new_row * GRID_WIDE + new_col, 0, TILES - 1)
        linked = inside[None, :] & present & present[:, target]
        columns.append(jnp.where(linked, target[None, :], -1))
    return jnp.stack(columns, axis=-1).astype(jnp.int32)


def draw_activations(key, part):
    key = jax.random.fold_in(key, 21)
    noise_key, tile_key = jax.random.split(key, 2)
    shape = (SLIDES, TILES, TILE_SIDE, TILE_SIDE, CH)
    tile_part = jnp.clip(jax.random.normal(tile_key, (SLIDES, TILES, 1, 1, CH), jnp.float32), -2.5, 2.5)
    noise = jnp.clip(jax.random.normal(noise_key, shape, jnp.float32), -4.0, 4.0)
    values = noise + tile_part
    return values.astype(jnp.bfloat16)


def draw_cotangent(key, part):
    key = jax.random.fold_in(key, 23)
    noise_key, mean_key, level_key = jax.random.split(key, 3)
    shape = (SLIDES, TILES, TILE_SIDE, TILE_SIDE, OUT_CH)
    mean_vec = 0.8 * jnp.clip(jax.random.normal(mean_key, (OUT_CH,), jnp.float32), -3.0, 3.0)
    level = jax.random.uniform(level_key, (SLIDES, TILES, 1, 1, 1), jnp.float32, 0.3, 1.2)
    noise = jnp.clip(jax.random.normal(noise_key, shape, jnp.float32), -4.0, 4.0)
    values = noise + level * mean_vec
    return values.astype(jnp.bfloat16)


def normal_values(key, extent, scale, bound, kind=jnp.bfloat16):
    drawn = jax.random.normal(key, extent, jnp.float32) * scale
    return jnp.minimum(jnp.maximum(drawn, -bound), bound).astype(kind)


def setup_inputs(seed: int = 0) -> dict:
    streams_of = jax.random.split(jax.random.key(seed), 10)
    activations = draw_activations(jax.random.fold_in(streams_of[9], 71), 0)
    tissue = draw_tissue(jax.random.fold_in(streams_of[9], 71), 0)
    neighbours = draw_neighbours(jax.random.fold_in(streams_of[9], 71), 0)
    w_reduce = normal_values(streams_of[3], (CH, CH), CH ** -0.5, 0.375)
    w_group = normal_values(streams_of[4], (3, 3, GROUP_WIDTH, CH), (9 * GROUP_WIDTH) ** -0.5, 0.75)
    norm_gain = jnp.clip(1.0 + 0.15 * jax.random.normal(streams_of[5], (CH,), jnp.float32), 0.25, 1.75)
    norm_bias = normal_values(streams_of[6], (CH,), 0.5, 3.0, jnp.float32)
    w_expand = normal_values(streams_of[7], (CH, OUT_CH), CH ** -0.5, 0.375)
    cotangent = draw_cotangent(jax.random.fold_in(streams_of[9], 71), 0)
    return dict(activations=activations, tissue=tissue, neighbours=neighbours, w_reduce=w_reduce, w_group=w_group, norm_gain=norm_gain, norm_bias=norm_bias, w_expand=w_expand, cotangent=cotangent)


epsilon = 1e-05

def extend(values, link_ids):
    top_rows = values[:, 0]
    bottom_rows = values[:, -1]
    left_cols = values[:, :, 0]
    right_cols = values[:, :, -1]

    def pick(strips, column):
        wanted = link_ids[:, column]
        taken = strips[jnp.clip(wanted, 0, strips.shape[0] - 1)]
        return jnp.where((wanted >= 0)[:, None, None], taken, jnp.zeros_like(taken))
    above = pick(bottom_rows, 0)
    below = pick(top_rows, 1)
    left_side = pick(right_cols, 2)
    right_side = pick(left_cols, 3)
    corner_nw = pick(bottom_rows, 4)[:, -1]
    corner_ne = pick(bottom_rows, 5)[:, 0]
    corner_sw = pick(top_rows, 6)[:, -1]
    corner_se = pick(top_rows, 7)[:, 0]
    upper = jnp.concatenate([corner_nw[:, None], above, corner_ne[:, None]], axis=1)
    lower = jnp.concatenate([corner_sw[:, None], below, corner_se[:, None]], axis=1)
    middle = jnp.concatenate([left_side[:, :, None], values, right_side[:, :, None]], axis=2)
    return jnp.concatenate([upper[:, None], middle, lower[:, None]], axis=1)

def grouped(padded, kernel):
    return lax.conv_general_dilated(padded, kernel, (1, 1), 'VALID', dimension_numbers=('NHWC', 'HWIO', 'NHWC'), feature_group_count=padded.shape[-1] // kernel.shape[2], preferred_element_type=jnp.float32)

def flipped(kernel):
    group_width = kernel.shape[2]
    width = kernel.shape[3]
    split = kernel.reshape(3, 3, group_width, width // group_width, group_width)[::-1, ::-1]
    return split.transpose(0, 1, 4, 3, 2).reshape(3, 3, group_width, width)

def kernel_grad(padded, grad, group_width):
    side = grad.shape[1]
    width = grad.shape[3]
    groups = width // group_width
    grad_groups = grad.reshape(-1, groups, group_width).astype(jnp.float32)
    rows_out = []
    for row_tap in range(3):
        cols_out = []
        for col_tap in range(3):
            window = padded[:, row_tap:row_tap + side, col_tap:col_tap + side, :].reshape(-1, groups, group_width).astype(jnp.float32)
            term = jnp.einsum('pgi,pgj->igj', window, grad_groups)
            cols_out.append(term.reshape(group_width, width))
        rows_out.append(jnp.stack(cols_out))
    return jnp.stack(rows_out)

def reduce_slab(slab, w_reduce):
    flat_input = slab.reshape(-1, slab.shape[-1])
    return jnp.dot(flat_input, w_reduce, preferred_element_type=jnp.float32).astype(jnp.bfloat16).reshape(slab.shape)

def reference(activations, tissue, neighbours, w_reduce, w_group, norm_gain, norm_bias, w_expand, cotangent):

    def forward_slide(pair):
        slab, link_ids = pair
        return grouped(extend(reduce_slab(slab, w_reduce), link_ids), w_group)
    pre_norm = lax.map(forward_slide, (activations, neighbours))
    weight = tissue.astype(jnp.float32)[..., None]
    counted = jnp.sum(tissue.astype(jnp.float32))
    centre = lax.optimization_barrier(jnp.sum(weight * pre_norm, axis=(0, 1, 2, 3))) / counted
    spread = lax.optimization_barrier(jnp.sum(weight * (pre_norm - centre) ** 2, axis=(0, 1, 2, 3))) / counted
    inverse_std = lax.rsqrt(spread + epsilon)

    def head(pre_slab, tissue_slab, grad_slab):
        normed = (pre_slab - centre) * inverse_std
        before = norm_gain * normed + norm_bias
        sigma = jax.nn.sigmoid(before)
        hidden = (before * sigma).astype(jnp.bfloat16)
        out_grad = grad_slab * tissue_slab[..., None].astype(jnp.bfloat16)
        out_flat = out_grad.reshape(-1, out_grad.shape[-1])
        hidden_grad = jnp.dot(out_flat, w_expand.T, preferred_element_type=jnp.float32).reshape(pre_slab.shape)
        before_grad = hidden_grad * sigma * (1.0 + before * (1.0 - sigma))
        return (normed, hidden, out_flat, before_grad)

    def first_pass(carry, items):
        pre_slab, tissue_slab, grad_slab = items
        normed, hidden, out_flat, before_grad = head(pre_slab, tissue_slab, grad_slab)
        hidden_flat = hidden.reshape(-1, hidden.shape[-1])
        expand_term = jnp.dot(hidden_flat.T, out_flat, preferred_element_type=jnp.float32)
        return ((carry[0] + expand_term, carry[1] + lax.optimization_barrier(jnp.sum(before_grad * normed, axis=(0, 1, 2))), carry[2] + lax.optimization_barrier(jnp.sum(before_grad, axis=(0, 1, 2)))), None)
    start = (jnp.zeros((w_expand.shape[0], w_expand.shape[1]), jnp.float32), jnp.zeros(norm_gain.shape, jnp.float32), jnp.zeros(norm_gain.shape, jnp.float32))
    (expand_grad, gain_grad, bias_grad), unused = lax.scan(first_pass, start, (pre_norm, tissue, cotangent))
    back_kernel = flipped(w_group)

    def second_pass(carry, items):
        slab, link_ids, pre_slab, tissue_slab, grad_slab = items
        normed, hidden, out_flat, before_grad = head(pre_slab, tissue_slab, grad_slab)
        tissue_weight = tissue_slab.astype(jnp.float32)[..., None]
        norm_grad = (norm_gain * inverse_std * (before_grad - tissue_weight * (bias_grad + normed * gain_grad) / counted)).astype(jnp.bfloat16)
        padded = extend(reduce_slab(slab, w_reduce), link_ids)
        padded_grad = extend(norm_grad, link_ids)
        reduced_grad = grouped(padded_grad, back_kernel).astype(jnp.bfloat16)
        group_term = kernel_grad(padded, norm_grad, w_group.shape[2])
        grad_flat = reduced_grad.reshape(-1, reduced_grad.shape[-1])
        flat_input = slab.reshape(-1, slab.shape[-1])
        reduce_term = jnp.dot(flat_input.T, grad_flat, preferred_element_type=jnp.float32)
        input_grad = jnp.dot(grad_flat, w_reduce.T, preferred_element_type=jnp.float32).astype(jnp.bfloat16).reshape(slab.shape)
        return ((carry[0] + reduce_term, carry[1] + group_term), input_grad)
    start_two = (jnp.zeros(w_reduce.shape, jnp.float32), jnp.zeros(w_group.shape, jnp.float32))
    (reduce_grad, group_grad), input_grad = lax.scan(second_pass, start_two, (activations, neighbours, pre_norm, tissue, cotangent))
    return (input_grad, reduce_grad, group_grad, gain_grad, bias_grad, expand_grad)
```

```python
import functools

import jax
import jax.numpy as jnp
from jax import lax
from jax.experimental import pallas as pl
from jax.experimental.pallas import tpu as pltpu
from jax.sharding import PartitionSpec as P

EPS = 1e-05
SIDE = 14
WIDE = 16
TILE_ROWS = SIDE * WIDE
ROWS = 2 * TILE_ROWS
EXT = WIDE * WIDE
CH = 256
OUT = 512
F32 = jnp.float32
BF16 = jnp.bfloat16

VMEM = pl.BlockSpec(memory_space=pltpu.VMEM)
SMEM = pl.BlockSpec(memory_space=pltpu.SMEM)
PARAMS = pltpu.CompilerParams(vmem_limit_bytes=24 * 1024 * 1024)


def call(kernel, outs, specs, scratch=()):
    return pl.pallas_call(
        kernel,
        out_shape=outs,
        in_specs=specs,
        out_specs=jax.tree.map(lambda _: VMEM, outs),
        scratch_shapes=scratch,
        compiler_params=PARAMS,
    )


def shape(dims, kind):
    return jax.ShapeDtypeStruct(dims, kind)


def dot(a, b, dims=((1,), (0,))):
    return lax.dot_general(a, b, (dims, ((), ())), preferred_element_type=F32)


def iota(dims, axis):
    return lax.broadcasted_iota(jnp.int32, dims, axis)


def rims_of(values, top_ref, bottom_ref):
    for t in range(2):
        first = t * TILE_ROWS
        last = first + TILE_ROWS - WIDE
        top_ref[t * WIDE : (t + 1) * WIDE] = values[first : first + WIDE]
        bottom_ref[t * WIDE : (t + 1) * WIDE] = values[last : last + WIDE]


def strips(values, up, down):
    out = []
    for t in range(2):
        out.append(
            jnp.concatenate(
                [
                    up[t * WIDE : (t + 1) * WIDE],
                    values[t * TILE_ROWS : (t + 1) * TILE_ROWS],
                    down[t * WIDE : (t + 1) * WIDE],
                ],
                axis=0,
            )
        )
    return out


def column_kernel(odd_ref, values_ref, up_ref, down_ref, column_ref):
    left, right = strips(values_ref[...], up_ref[...], down_ref[...])
    row = iota((WIDE, EXT), 0)
    place = iota((WIDE, EXT), 1)
    odd = odd_ref[0] == 1
    wanted = row * WIDE + jnp.where(odd, 0, SIDE - 1)
    pick = (place == wanted).astype(F32).astype(BF16)
    from_left = dot(pick, left)
    from_right = dot(pick, right)
    column_ref[...] = jnp.where(odd, from_left, from_right).astype(BF16)


def extended(values, up, down, side, links_ref):
    left, right = strips(values.astype(F32), up.astype(F32), down.astype(F32))
    r = iota((EXT, CH), 0) // WIDE
    c = iota((EXT, CH), 0) % WIDE
    spread_row = iota((EXT, WIDE), 0) // WIDE
    spread = (spread_row == iota((EXT, WIDE), 1)).astype(F32).astype(BF16)
    side_rows = dot(spread, side)

    def gate(t, first, middle, last):
        def on(k):
            return (links_ref[0, t, k] >= 0).astype(jnp.int32)

        level = jnp.where(r == 0, on(first), jnp.where(r == WIDE - 1, on(last), on(middle)))
        return level > 0

    out = []
    for t, own, other in ((0, left, right), (1, right, left)):
        keep = jnp.where(r == 0, (links_ref[0, t, 0] >= 0).astype(jnp.int32), 1)
        keep = jnp.where(r == WIDE - 1, (links_ref[0, t, 1] >= 0).astype(jnp.int32), keep)
        centre = pltpu.roll(jnp.where(keep > 0, own, 0.0), 1, 0)
        at_left = side_rows if t == 0 else pltpu.roll(other, EXT - (SIDE - 1), 0)
        at_right = pltpu.roll(other, WIDE - 1, 0) if t == 0 else side_rows
        value = jnp.where(c == 0, jnp.where(gate(t, 4, 2, 6), at_left, 0.0), centre)
        value = jnp.where(c == WIDE - 1, jnp.where(gate(t, 5, 3, 7), at_right, 0.0), value)
        out.append(value)
    return out


def shifted(tiles):
    moved = []
    for b in range(3):
        moved.append([(t if b == 0 else pltpu.roll(t, EXT - b, 0)).astype(BF16) for t in tiles])
    return moved


def window(moved, a, b):
    return jnp.concatenate([t[a * WIDE : a * WIDE + TILE_ROWS] for t in moved[b]], axis=0)


def reduce_kernel(act_ref, w_ref, tissue_ref, values_ref, top_ref, bottom_ref, mask_ref, wide):
    wide[...] = jnp.zeros_like(wide)
    wide[:, :, :SIDE, :] = act_ref[0]
    values = dot(wide[...].reshape(ROWS, CH), w_ref[...]).astype(BF16)
    values_ref[...] = values
    rims_of(values, top_ref, bottom_ref)
    row = iota((TILE_ROWS, SIDE), 0) // WIDE
    pick = (row == iota((TILE_ROWS, SIDE), 1)).astype(F32).astype(BF16)
    col = iota((TILE_ROWS, SIDE), 0) % WIDE
    here = col == iota((TILE_ROWS, SIDE), 1)
    ones = jnp.ones((SIDE, 128), BF16)
    for t in range(2):
        rows = dot(pick, tissue_ref[0, t].astype(F32).astype(BF16))
        mask_ref[t * TILE_ROWS : (t + 1) * TILE_ROWS] = dot(
            jnp.where(here, rows, 0.0).astype(BF16), ones
        )


def spread_kernel(group_ref, dense_ref):
    same = iota((CH, CH), 0) // 8 == iota((CH, CH), 1) // 8
    for tap in range(9):
        taps = group_ref[tap // 3, tap % 3].astype(F32)
        full = jnp.concatenate([taps] * (CH // 8), axis=0)
        dense_ref[tap] = jnp.where(same, full, 0.0).astype(BF16)


def as_rows(first, second, third):
    pieces = [first[:, :128], first[:, 128:], second[:, :128], second[:, 128:], third]
    return jnp.concatenate(pieces + [jnp.zeros((3, 128), F32)], axis=0)


def per_channel(block, row):
    return jnp.concatenate([block[row : row + 1], block[row + 1 : row + 2]], axis=1)


def both(mask):
    return jnp.concatenate([mask, mask], axis=1)


def conv_kernel(
    links_ref, values_ref, up_ref, down_ref, side_ref, dense_ref, mask_ref,
    pre_ref, padded_ref, sums_ref,
):
    tiles = extended(values_ref[...], up_ref[...], down_ref[...], side_ref[...], links_ref)
    for t in range(2):
        padded_ref[t] = tiles[t].astype(BF16)
    moved = shifted(tiles)
    pre = jnp.zeros((ROWS, CH), F32)
    for a in range(3):
        for b in range(3):
            pre += dot(window(moved, a, b), dense_ref[3 * a + b])
    pre_ref[...] = pre
    mask = mask_ref[...]
    held = pre * both(mask)
    block = as_rows(
        jnp.sum(held, axis=0, keepdims=True),
        jnp.sum(held * pre, axis=0, keepdims=True),
        jnp.sum(mask, axis=0, keepdims=True),
    )
    sums_ref[...] = jnp.broadcast_to(block[None], sums_ref.shape)


def between_kernel(parts_ref, sums_ref):
    block = jnp.sum(parts_ref[...], axis=0)
    sums_ref[...] = jnp.broadcast_to(block[None], sums_ref.shape)


def moments(parts_ref):
    block = jnp.sum(parts_ref[...], axis=0)
    counted = both(block[4:5])
    centre = per_channel(block, 0) / counted
    spread = per_channel(block, 2) / counted - centre * centre
    return centre, lax.rsqrt(spread + EPS), counted


def head_kernel(
    parts_ref, pre_ref, mask_ref, gain_ref, bias_ref, expand_ref, cot_ref,
    before_ref, expand_grad_ref, sums_ref, wide,
):
    wide[...] = jnp.zeros_like(wide)
    wide[:, :, :SIDE, :] = cot_ref[0]
    mask = mask_ref[...]
    keep = jnp.concatenate([mask] * (OUT // 128), axis=1) > 0
    out_grad = jnp.where(keep, wide[...].reshape(ROWS, OUT).astype(F32), 0.0).astype(BF16)
    centre, inverse, _ = moments(parts_ref)
    normed = (pre_ref[...] - centre) * inverse
    before = gain_ref[...] * normed + bias_ref[...]
    sigma = jax.nn.sigmoid(before)
    hidden = (before * sigma).astype(BF16)
    expand_grad_ref[...] = dot(hidden, out_grad, ((0,), (0,)))
    hidden_grad = dot(out_grad, expand_ref[...], ((1,), (1,)))
    before_grad = hidden_grad * sigma * (1.0 + before * (1.0 - sigma))
    before_ref[...] = before_grad
    block = as_rows(
        jnp.sum(before_grad * normed, axis=0, keepdims=True),
        jnp.sum(before_grad, axis=0, keepdims=True),
        jnp.zeros((1, 128), F32),
    )
    sums_ref[...] = jnp.broadcast_to(block[None], sums_ref.shape)


def norm_kernel(
    parts_ref, totals_ref, pre_ref, mask_ref, gain_ref, before_ref,
    grad_ref, top_ref, bottom_ref, gain_grad_ref, bias_grad_ref,
):
    centre, inverse, counted = moments(parts_ref)
    totals = jnp.sum(totals_ref[...], axis=0)
    gain_grad = per_channel(totals, 0)
    bias_grad = per_channel(totals, 2)
    gain_grad_ref[...] = gain_grad
    bias_grad_ref[...] = bias_grad
    normed = (pre_ref[...] - centre) * inverse
    taken = both(mask_ref[...]) * (bias_grad + normed * gain_grad) / counted
    grad = (gain_ref[...] * inverse * (before_ref[...] - taken)).astype(BF16)
    grad_ref[...] = grad
    rims_of(grad, top_ref, bottom_ref)


def back_kernel(
    links_ref, grad_ref, up_ref, down_ref, side_ref, dense_ref, padded_ref, act_ref, w_ref,
    expand_grad_ref, input_grad_ref, packed_ref, wide,
):
    wide[...] = jnp.zeros_like(wide)
    wide[:, :, :SIDE, :] = act_ref[0]
    act = wide[...].reshape(ROWS, CH)
    grad = grad_ref[...]
    moved = shifted(extended(grad, up_ref[...], down_ref[...], side_ref[...], links_ref))
    reduced = jnp.zeros((ROWS, CH), F32)
    for a in range(3):
        for b in range(3):
            reduced += dot(window(moved, a, b), dense_ref[8 - 3 * a - b], ((1,), (1,)))
    in_tile = iota((ROWS, CH), 0) % WIDE < SIDE
    reduced = jnp.where(in_tile, reduced, 0.0).astype(BF16)
    input_grad = dot(reduced, w_ref[...], ((1,), (1,))).astype(BF16)
    input_grad_ref[0] = input_grad.reshape(2, SIDE, WIDE, CH)[:, :, :SIDE, :]
    reduce_grad = dot(act, reduced, ((0,), (0,))).astype(BF16)
    packed_ref[:CH, :128] = reduce_grad[:, :128]
    packed_ref[CH:, :128] = reduce_grad[:, 128:]
    expand_grad = expand_grad_ref[...].astype(BF16)
    packed_ref[:CH, 128:256] = expand_grad[:, :128]
    packed_ref[CH:, 128:256] = expand_grad[:, 128:256]
    packed_ref[:CH, 256:384] = expand_grad[:, 256:384]
    packed_ref[CH:, 256:384] = expand_grad[:, 384:]
    lowered = []
    for a in range(3):
        parts = []
        for t in range(2):
            own = grad[t * TILE_ROWS : (t + 1) * TILE_ROWS]
            if a:
                parts.append(jnp.zeros((a * WIDE, CH), BF16))
            parts.append(own)
            if a < 2:
                parts.append(jnp.zeros(((2 - a) * WIDE, CH), BF16))
        lowered.append(jnp.concatenate(parts, axis=0))
    lowered = jnp.concatenate(lowered, axis=1)
    windows = shifted([padded_ref[t].astype(F32) for t in range(2)])
    same = iota((CH, CH), 0) // 8 == iota((CH, CH), 1) // 8
    taps = [None] * 9
    for b in range(3):
        product = dot(jnp.concatenate(windows[b], axis=0), lowered, ((0,), (0,)))
        for a in range(3):
            own = jnp.where(same, product[:, a * CH : (a + 1) * CH], 0.0)
            taps[3 * a + b] = jnp.sum(own.reshape(CH // 8, 8, CH), axis=0)
    group = jnp.concatenate(taps + [jnp.zeros((CH - 72, CH), F32)], axis=0).astype(BF16)
    packed_ref[:CH, 384:] = group[:, :128]
    packed_ref[CH:, 384:] = group[:, 128:]


def total_kernel(parts_ref, total_ref):
    ones = jnp.ones(total_ref.shape[:1] + parts_ref.shape[:1], BF16)
    total_ref[...] = dot(ones, parts_ref[...]).astype(BF16)


def unpack_kernel(packed_ref, reduce_ref, group_ref, expand_ref):
    packed = packed_ref[...].astype(F32)
    reduce_ref[:, :128] = packed[:CH, :128]
    reduce_ref[:, 128:] = packed[CH:, :128]
    expand_ref[:, :128] = packed[:CH, 128:256]
    expand_ref[:, 128:256] = packed[CH:, 128:256]
    expand_ref[:, 256:384] = packed[:CH, 256:384]
    expand_ref[:, 384:] = packed[CH:, 256:384]
    group_ref[:, :128] = packed[:72, 384:]
    group_ref[:, 128:] = packed[CH : CH + 72, 384:]


def body(
    sizes, activations, tissue, neighbours, w_reduce, w_group, norm_gain, norm_bias, w_expand,
    cotangent,
):
    dp, space = sizes
    everyone = ("dp", "space")
    odd = (lax.axis_index("space") % 2).astype(jnp.int32).reshape(1)
    gain = norm_gain.reshape(1, CH)
    bias = norm_bias.reshape(1, CH)
    rim = shape((2 * WIDE, CH), BF16)
    flat = shape((ROWS, CH), BF16)

    def halo(values, top, bottom):
        up = lax.ppermute(bottom, "space", [(i, i + 2) for i in range(space - 2)])
        down = lax.ppermute(top, "space", [(i + 2, i) for i in range(space - 2)])
        column = call(
            column_kernel, shape((WIDE, CH), BF16), [SMEM, VMEM, VMEM, VMEM]
        )(odd, values, up, down)
        side = lax.ppermute(column, "space", [(i, i ^ 1) for i in range(space)])
        return up, down, side

    def summed(blocks):
        parts = lax.all_to_all(blocks, "space", 0, 0)
        blocks = call(between_kernel, shape((dp, 8, 128), F32), [VMEM])(parts)
        return lax.all_to_all(blocks, "dp", 0, 0)

    values, top, bottom, mask = call(
        reduce_kernel,
        (flat, rim, rim, shape((ROWS, 128), F32)),
        [VMEM] * 3,
        [pltpu.VMEM((2, SIDE, WIDE, CH), BF16)],
    )(activations, w_reduce, tissue)
    dense = call(spread_kernel, shape((9, CH, CH), BF16), [VMEM])(w_group)
    up, down, side = halo(values, top, bottom)
    blocks = shape((space, 8, 128), F32)
    pre, padded, sums = call(
        conv_kernel,
        (shape((ROWS, CH), F32), shape((2, EXT, CH), BF16), blocks),
        [SMEM] + [VMEM] * 6,
    )(neighbours, values, up, down, side, dense, mask)
    parts = summed(sums)
    before_grad, expand_grad, sums = call(
        head_kernel,
        (shape((ROWS, CH), F32), shape((CH, OUT), F32), blocks),
        [VMEM] * 7,
        [pltpu.VMEM((2, SIDE, WIDE, OUT), BF16)],
    )(parts, pre, mask, gain, bias, w_expand, cotangent)
    totals = summed(sums)
    grad, top, bottom, gain_grad, bias_grad = call(
        norm_kernel,
        (flat, rim, rim, shape((1, CH), F32), shape((1, CH), F32)),
        [VMEM] * 6,
    )(parts, totals, pre, mask, gain, before_grad)
    up, down, side = halo(grad, top, bottom)
    count = dp * space
    input_grad, packed = call(
        back_kernel,
        (shape((1, 2, SIDE, SIDE, CH), BF16), shape((2 * CH, 4 * 128), BF16)),
        [SMEM] + [VMEM] * 9,
        [pltpu.VMEM((2, SIDE, WIDE, CH), BF16)],
    )(neighbours, grad, up, down, side, dense, padded, activations, w_reduce, expand_grad)
    share = packed.size // count
    received = lax.all_to_all(packed.reshape(count, 1, share), everyone, 0, 0)
    total = call(total_kernel, shape((count, share), BF16), [VMEM])(
        received.reshape(count, share)
    )
    gathered = lax.all_to_all(total.reshape(count, 1, share), everyone, 0, 0)
    reduce_grad, group_grad, expand_grad = call(
        unpack_kernel,
        (shape((CH, CH), F32), shape((72, CH), F32), shape((CH, OUT), F32)),
        [VMEM],
    )(gathered.reshape(packed.shape))
    return (
        input_grad,
        reduce_grad,
        group_grad.reshape(3, 3, 8, CH),
        gain_grad.reshape(CH),
        bias_grad.reshape(CH),
        expand_grad,
    )


def solution(mesh):
    sizes = (mesh.shape["dp"], mesh.shape["space"])
    return jax.shard_map(
        functools.partial(body, sizes),
        mesh=mesh,
        in_specs=(
            P("dp", "space", None, None, None),
            P("dp", "space", None, None),
            P("dp", "space", None),
            P(),
            P(),
            P(),
            P(),
            P(),
            P("dp", "space", None, None, None),
        ),
        out_specs=(P("dp", "space", None, None, None), P(), P(), P(), P(), P()),
        check_vma=False,
    )
```

```python
import functools

import jax
import jax.numpy as jnp
from jax import lax
from jax.experimental import pallas as pl
from jax.experimental.pallas import tpu as pltpu
from jax.sharding import Mesh
from jax.sharding import PartitionSpec as P

SPACE = ("long", "near")
FAR = ("dp", "long")
ALL = ("dp", "long", "near")
EPS = 1e-05
SIDE = 14
WIDE = 16
TILE_ROWS = SIDE * WIDE
ROWS = 2 * TILE_ROWS
EXT = WIDE * WIDE
CH = 256
OUT = 512
F32 = jnp.float32
BF16 = jnp.bfloat16

VMEM = pl.BlockSpec(memory_space=pltpu.VMEM)
SMEM = pl.BlockSpec(memory_space=pltpu.SMEM)
HBM = pl.BlockSpec(memory_space=pl.ANY)
PARAMS = pltpu.CompilerParams(vmem_limit_bytes=24 * 1024 * 1024)


def call(kernel, outs, specs, scratch=()):
    return pl.pallas_call(
        kernel,
        out_shape=outs,
        in_specs=specs,
        out_specs=jax.tree.map(lambda _: VMEM, outs),
        scratch_shapes=scratch,
        compiler_params=PARAMS,
    )


def shape(dims, kind):
    return jax.ShapeDtypeStruct(dims, kind)


def dot(a, b, dims=((1,), (0,))):
    return lax.dot_general(a, b, (dims, ((), ())), preferred_element_type=F32)


def iota(dims, axis):
    return lax.broadcasted_iota(jnp.int32, dims, axis)


def rims_of(values, top_ref, bottom_ref):
    for t in range(2):
        first = t * TILE_ROWS
        last = first + TILE_ROWS - WIDE
        top_ref[t * WIDE : (t + 1) * WIDE] = values[first : first + WIDE]
        bottom_ref[t * WIDE : (t + 1) * WIDE] = values[last : last + WIDE]


def strips(values, up, down):
    out = []
    for t in range(2):
        out.append(
            jnp.concatenate(
                [
                    up[t * WIDE : (t + 1) * WIDE],
                    values[t * TILE_ROWS : (t + 1) * TILE_ROWS],
                    down[t * WIDE : (t + 1) * WIDE],
                ],
                axis=0,
            )
        )
    return out


def column_kernel(odd_ref, values_ref, up_ref, down_ref, after_ref, column_ref):
    del after_ref
    left, right = strips(values_ref[...], up_ref[...], down_ref[...])
    row = iota((WIDE, EXT), 0)
    place = iota((WIDE, EXT), 1)
    odd = odd_ref[0] == 1
    wanted = row * WIDE + jnp.where(odd, 0, SIDE - 1)
    pick = (place == wanted).astype(F32).astype(BF16)
    from_left = dot(pick, left)
    from_right = dot(pick, right)
    column_ref[...] = jnp.where(odd, from_left, from_right).astype(BF16)


def extended(values, up, down, side, links_ref):
    left, right = strips(values.astype(F32), up.astype(F32), down.astype(F32))
    r = iota((EXT, CH), 0) // WIDE
    c = iota((EXT, CH), 0) % WIDE
    spread_row = iota((EXT, WIDE), 0) // WIDE
    spread = (spread_row == iota((EXT, WIDE), 1)).astype(F32).astype(BF16)
    side_rows = dot(spread, side)

    def gate(t, first, middle, last):
        def on(k):
            return (links_ref[0, t, k] >= 0).astype(jnp.int32)

        level = jnp.where(r == 0, on(first), jnp.where(r == WIDE - 1, on(last), on(middle)))
        return level > 0

    out = []
    for t, own, other in ((0, left, right), (1, right, left)):
        keep = jnp.where(r == 0, (links_ref[0, t, 0] >= 0).astype(jnp.int32), 1)
        keep = jnp.where(r == WIDE - 1, (links_ref[0, t, 1] >= 0).astype(jnp.int32), keep)
        centre = pltpu.roll(jnp.where(keep > 0, own, 0.0), 1, 0)
        at_left = side_rows if t == 0 else pltpu.roll(other, EXT - (SIDE - 1), 0)
        at_right = pltpu.roll(other, WIDE - 1, 0) if t == 0 else side_rows
        value = jnp.where(c == 0, jnp.where(gate(t, 4, 2, 6), at_left, 0.0), centre)
        value = jnp.where(c == WIDE - 1, jnp.where(gate(t, 5, 3, 7), at_right, 0.0), value)
        out.append(value)
    return out


def shifted(tiles):
    moved = []
    for b in range(3):
        moved.append([(t if b == 0 else pltpu.roll(t, EXT - b, 0)).astype(BF16) for t in tiles])
    return moved


def window(moved, a, b):
    return jnp.concatenate([t[a * WIDE : a * WIDE + TILE_ROWS] for t in moved[b]], axis=0)


def reduce_kernel(act_ref, w_ref, values_ref, top_ref, bottom_ref, wide):
    wide[...] = jnp.zeros_like(wide)
    wide[:, :, :SIDE, :] = act_ref[0]
    values = dot(wide[...].reshape(ROWS, CH), w_ref[...]).astype(BF16)
    values_ref[...] = values
    rims_of(values, top_ref, bottom_ref)


def prepare_kernel(
    tissue_ref, group_ref, cot_ref, expand_ref,
    mask_ref, dense_ref, out_grad_ref, hidden_grad_ref, wide,
):
    row = iota((TILE_ROWS, SIDE), 0) // WIDE
    pick = (row == iota((TILE_ROWS, SIDE), 1)).astype(F32).astype(BF16)
    col = iota((TILE_ROWS, SIDE), 0) % WIDE
    here = col == iota((TILE_ROWS, SIDE), 1)
    ones = jnp.ones((SIDE, 128), BF16)
    masks = []
    for t in range(2):
        rows = dot(pick, tissue_ref[0, t].astype(F32).astype(BF16))
        masks.append(dot(jnp.where(here, rows, 0.0).astype(BF16), ones))
    mask = jnp.concatenate(masks, axis=0)
    mask_ref[...] = mask
    same = iota((CH, CH), 0) // 8 == iota((CH, CH), 1) // 8
    for tap in range(9):
        taps = group_ref[tap // 3, tap % 3].astype(F32)
        full = jnp.concatenate([taps] * (CH // 8), axis=0)
        dense_ref[tap] = jnp.where(same, full, 0.0).astype(BF16)
    wide[...] = jnp.zeros_like(wide)
    wide[:, :, :SIDE, :] = cot_ref[0]
    keep = jnp.concatenate([mask] * (OUT // 128), axis=1) > 0
    out_grad = jnp.where(keep, wide[...].reshape(ROWS, OUT).astype(F32), 0.0).astype(BF16)
    out_grad_ref[...] = out_grad
    hidden_grad_ref[...] = dot(out_grad, expand_ref[...], ((1,), (1,)))


def both(mask):
    return jnp.concatenate([mask, mask], axis=1)


def conv_kernel(
    links_ref, values_ref, up_ref, down_ref, side_ref, dense_ref, mask_ref,
    pre_ref, padded_ref, sums_ref,
):
    tiles = extended(values_ref[...], up_ref[...], down_ref[...], side_ref[...], links_ref)
    for t in range(2):
        padded_ref[t] = tiles[t].astype(BF16)
    moved = shifted(tiles)
    pre = jnp.zeros((ROWS, CH), F32)
    for a in range(3):
        for b in range(3):
            pre += dot(window(moved, a, b), dense_ref[3 * a + b])
    pre_ref[...] = pre
    mask = mask_ref[...]
    held = pre * both(mask)
    block = jnp.concatenate(
        [
            jnp.sum(held, axis=0, keepdims=True),
            jnp.sum(held * pre, axis=0, keepdims=True),
            jnp.sum(mask, axis=0, keepdims=True),
        ],
        axis=1,
    )
    sums_ref[...] = jnp.broadcast_to(block[None], sums_ref.shape)


def between_kernel(parts_ref, sums_ref):
    block = jnp.sum(parts_ref[...], axis=0)
    sums_ref[...] = jnp.broadcast_to(block[None], sums_ref.shape)


def moments(parts_ref):
    block = jnp.sum(parts_ref[...], axis=0)
    counted = both(block[:, 2 * CH :])
    centre = block[:, :CH] / counted
    spread = block[:, CH : 2 * CH] / counted - centre * centre
    return centre, lax.rsqrt(spread + EPS), counted


def head_kernel(
    parts_ref, pre_ref, gain_ref, bias_ref, out_grad_ref, hidden_grad_ref,
    before_ref, expand_grad_ref, sums_ref,
):
    centre, inverse, _ = moments(parts_ref)
    normed = (pre_ref[...] - centre) * inverse
    before = gain_ref[...] * normed + bias_ref[...]
    sigma = jax.nn.sigmoid(before)
    hidden = (before * sigma).astype(BF16)
    expand_grad_ref[...] = dot(hidden, out_grad_ref[...], ((0,), (0,)))
    before_grad = hidden_grad_ref[...] * sigma * (1.0 + before * (1.0 - sigma))
    before_ref[...] = before_grad
    gain_grad = jnp.sum(before_grad * normed, axis=0, keepdims=True)
    bias_grad = jnp.sum(before_grad, axis=0, keepdims=True)
    block = jnp.concatenate([gain_grad, bias_grad], axis=1)
    sums_ref[...] = jnp.broadcast_to(block[None], sums_ref.shape)


def norm_kernel(
    parts_ref, totals_ref, pre_ref, mask_ref, gain_ref, before_ref,
    grad_ref, top_ref, bottom_ref, gain_grad_ref, bias_grad_ref,
):
    centre, inverse, counted = moments(parts_ref)
    totals = jnp.sum(totals_ref[...], axis=0)
    gain_grad = totals[:, :CH]
    bias_grad = totals[:, CH:]
    gain_grad_ref[...] = gain_grad
    bias_grad_ref[...] = bias_grad
    normed = (pre_ref[...] - centre) * inverse
    taken = both(mask_ref[...]) * (bias_grad + normed * gain_grad) / counted
    grad = (gain_ref[...] * inverse * (before_ref[...] - taken)).astype(BF16)
    grad_ref[...] = grad
    rims_of(grad, top_ref, bottom_ref)


def back_kernel(
    links_ref, grad_ref, up_ref, down_ref, side_ref, dense_ref, padded_ref, act_ref, w_ref,
    expand_grad_ref, input_grad_ref, packed_ref, wide,
):
    wide[...] = jnp.zeros_like(wide)
    wide[:, :, :SIDE, :] = act_ref[0]
    act = wide[...].reshape(ROWS, CH)
    grad = grad_ref[...]
    moved = shifted(extended(grad, up_ref[...], down_ref[...], side_ref[...], links_ref))
    reduced = jnp.zeros((ROWS, CH), F32)
    for a in range(3):
        for b in range(3):
            reduced += dot(window(moved, a, b), dense_ref[8 - 3 * a - b], ((1,), (1,)))
    in_tile = iota((ROWS, CH), 0) % WIDE < SIDE
    reduced = jnp.where(in_tile, reduced, 0.0).astype(BF16)
    input_grad = dot(reduced, w_ref[...], ((1,), (1,))).astype(BF16)
    input_grad_ref[0] = input_grad.reshape(2, SIDE, WIDE, CH)[:, :, :SIDE, :]
    reduce_grad = dot(act, reduced, ((0,), (0,))).astype(BF16)
    packed_ref[:CH] = reduce_grad
    expand_grad = expand_grad_ref[...].astype(BF16)
    packed_ref[CH : 2 * CH] = expand_grad[:, :CH]
    packed_ref[2 * CH : 3 * CH] = expand_grad[:, CH:]
    lowered = []
    for a in range(3):
        parts = []
        for t in range(2):
            own = grad[t * TILE_ROWS : (t + 1) * TILE_ROWS]
            if a:
                parts.append(jnp.zeros((a * WIDE, CH), BF16))
            parts.append(own)
            if a < 2:
                parts.append(jnp.zeros(((2 - a) * WIDE, CH), BF16))
        lowered.append(jnp.concatenate(parts, axis=0))
    lowered = jnp.concatenate(lowered, axis=1)
    windows = shifted([padded_ref[t].astype(F32) for t in range(2)])
    same = iota((CH, CH), 0) // 8 == iota((CH, CH), 1) // 8
    taps = [None] * 9
    for b in range(3):
        product = dot(jnp.concatenate(windows[b], axis=0), lowered, ((0,), (0,)))
        for a in range(3):
            own = jnp.where(same, product[:, a * CH : (a + 1) * CH], 0.0)
            taps[3 * a + b] = jnp.sum(own.reshape(CH // 8, 8, CH), axis=0)
    group = jnp.concatenate(taps + [jnp.zeros((CH - 72, CH), F32)], axis=0).astype(BF16)
    packed_ref[3 * CH :] = group


def total_kernel(parts_ref, total_ref):
    rows = parts_ref.shape[0]
    own = total_ref.shape[1]
    pick = iota((own, rows), 1) % own == iota((own, rows), 0)
    total = dot(pick.astype(F32).astype(BF16), parts_ref[...]).astype(BF16)
    total_ref[...] = jnp.broadcast_to(total[None], total_ref.shape)


def unpack_kernel(packed_ref, reduce_ref, group_ref, expand_ref):
    packed = packed_ref[...].astype(F32)
    reduce_ref[...] = packed[:CH]
    expand_ref[:, :CH] = packed[CH : 2 * CH]
    expand_ref[:, CH:] = packed[2 * CH : 3 * CH]
    group_ref[...] = packed[3 * CH : 3 * CH + 72]


def body(
    sizes, activations, tissue, neighbours, w_reduce, w_group, norm_gain, norm_bias, w_expand,
    cotangent,
):
    dp, long, near = sizes
    space = long * near
    odd = (lax.axis_index(SPACE) % 2).astype(jnp.int32).reshape(1)
    gain = norm_gain.reshape(1, CH)
    bias = norm_bias.reshape(1, CH)
    rim = shape((2 * WIDE, CH), BF16)
    flat = shape((ROWS, CH), BF16)
    full = shape((ROWS, CH), F32)

    def halo(values, top, bottom, after):
        up = lax.ppermute(bottom, SPACE, [(i, i + 2) for i in range(space - 2)])
        down = lax.ppermute(top, SPACE, [(i + 2, i) for i in range(space - 2)])
        column = call(
            column_kernel, shape((WIDE, CH), BF16), [SMEM] + [VMEM] * 3 + [HBM]
        )(odd, values, up, down, after)
        side = lax.ppermute(column, SPACE, [(i, i ^ 1) for i in range(space)])
        return up, down, side

    def summed(blocks):
        parts = lax.all_to_all(blocks, "near", 0, 0)
        blocks = call(
            between_kernel, shape((dp * long,) + blocks.shape[1:], F32), [VMEM]
        )(parts)
        return lax.all_to_all(blocks, FAR, 0, 0)

    values, top, bottom = call(
        reduce_kernel, (flat, rim, rim), [VMEM] * 2, [pltpu.VMEM((2, SIDE, WIDE, CH), BF16)]
    )(activations, w_reduce)
    mask, dense, out_grad, hidden_grad = call(
        prepare_kernel,
        (
            shape((ROWS, 128), F32),
            shape((9, CH, CH), BF16),
            shape((ROWS, OUT), BF16),
            full,
        ),
        [VMEM] * 4,
        [pltpu.VMEM((2, SIDE, WIDE, OUT), BF16)],
    )(tissue, w_group, cotangent, w_expand)
    up, down, side = halo(values, top, bottom, mask)
    pre, padded, sums = call(
        conv_kernel,
        (full, shape((2, EXT, CH), BF16), shape((near, 1, 2 * CH + 128), F32)),
        [SMEM] + [VMEM] * 6,
    )(neighbours, values, up, down, side, dense, mask)
    parts = summed(sums)
    before_grad, expand_grad, sums = call(
        head_kernel,
        (full, shape((CH, OUT), F32), shape((near, 1, 2 * CH), F32)),
        [VMEM] * 6,
    )(parts, pre, gain, bias, out_grad, hidden_grad)
    totals = summed(sums)
    grad, top, bottom, gain_grad, bias_grad = call(
        norm_kernel,
        (flat, rim, rim, shape((1, CH), F32), shape((1, CH), F32)),
        [VMEM] * 6,
    )(parts, totals, pre, mask, gain, before_grad)
    up, down, side = halo(grad, top, bottom, mask)
    input_grad, packed = call(
        back_kernel,
        (shape((1, 2, SIDE, SIDE, CH), BF16), shape((4 * CH, CH), BF16)),
        [SMEM] + [VMEM] * 9,
        [pltpu.VMEM((2, SIDE, WIDE, CH), BF16)],
    )(neighbours, grad, up, down, side, dense, padded, activations, w_reduce, expand_grad)
    count = dp * space
    shares = (count, packed.shape[0] // count, CH)
    received = lax.all_to_all(packed.reshape(shares), ALL, 0, 0)
    total = call(total_kernel, shape(shares, BF16), [VMEM])(received.reshape(packed.shape))
    gathered = lax.all_to_all(total, ALL, 0, 0)
    reduce_grad, group_grad, expand_grad = call(
        unpack_kernel,
        (shape((CH, CH), F32), shape((72, CH), F32), shape((CH, OUT), F32)),
        [VMEM],
    )(gathered.reshape(packed.shape))
    return (
        input_grad,
        reduce_grad,
        group_grad.reshape(3, 3, 8, CH),
        gain_grad.reshape(CH),
        bias_grad.reshape(CH),
        expand_grad,
    )


def solution(mesh):
    dp = mesh.shape["dp"]
    near = min(16, mesh.shape["space"])
    long = mesh.shape["space"] // near
    cut = Mesh(mesh.devices.reshape(dp, long, near), ("dp", "long", "near"))
    return jax.shard_map(
        functools.partial(body, (dp, long, near)),
        mesh=cut,
        in_specs=(
            P("dp", SPACE, None, None, None),
            P("dp", SPACE, None, None),
            P("dp", SPACE, None),
            P(),
            P(),
            P(),
            P(),
            P(),
            P("dp", SPACE, None, None, None),
        ),
        out_specs=(P("dp", SPACE, None, None, None), P(), P(), P(), P(), P()),
        check_vma=False,
    )
```

```python
import functools

import jax
import jax.numpy as jnp
from jax import lax
from jax.experimental import pallas as pl
from jax.experimental.pallas import tpu as pltpu
from jax.sharding import Mesh
from jax.sharding import PartitionSpec as P

SPACE = ("long", "near")
FAR = ("dp", "long")
ALL = ("dp", "long", "near")
EPS = 1e-05
SIDE = 14
WIDE = 16
TILE_ROWS = SIDE * WIDE
ROWS = 2 * TILE_ROWS
EXT = WIDE * WIDE
CH = 256
OUT = 512
F32 = jnp.float32
BF16 = jnp.bfloat16

VMEM = pl.BlockSpec(memory_space=pltpu.VMEM)
SMEM = pl.BlockSpec(memory_space=pltpu.SMEM)
HBM = pl.BlockSpec(memory_space=pl.ANY)
PARAMS = pltpu.CompilerParams(vmem_limit_bytes=24 * 1024 * 1024)


def call(kernel, outs, specs, scratch=()):
    return pl.pallas_call(
        kernel,
        out_shape=outs,
        in_specs=specs,
        out_specs=jax.tree.map(lambda _: VMEM, outs),
        scratch_shapes=scratch,
        compiler_params=PARAMS,
    )


def shape(dims, kind):
    return jax.ShapeDtypeStruct(dims, kind)


def dot(a, b, dims=((1,), (0,))):
    return lax.dot_general(a, b, (dims, ((), ())), preferred_element_type=F32)


def iota(dims, axis):
    return lax.broadcasted_iota(jnp.int32, dims, axis)


def rims_of(values, top_ref, bottom_ref):
    for t in range(2):
        first = t * TILE_ROWS
        last = first + TILE_ROWS - WIDE
        top_ref[t * WIDE : (t + 1) * WIDE] = values[first : first + WIDE]
        bottom_ref[t * WIDE : (t + 1) * WIDE] = values[last : last + WIDE]


def strips(values, up, down):
    out = []
    for t in range(2):
        out.append(
            jnp.concatenate(
                [
                    up[t * WIDE : (t + 1) * WIDE],
                    values[t * TILE_ROWS : (t + 1) * TILE_ROWS],
                    down[t * WIDE : (t + 1) * WIDE],
                ],
                axis=0,
            )
        )
    return out


def column_kernel(odd_ref, values_ref, up_ref, down_ref, after_ref, column_ref):
    del after_ref
    left, right = strips(values_ref[...], up_ref[...], down_ref[...])
    row = iota((WIDE, EXT), 0)
    place = iota((WIDE, EXT), 1)
    odd = odd_ref[0] == 1
    wanted = row * WIDE + jnp.where(odd, 0, SIDE - 1)
    pick = (place == wanted).astype(F32).astype(BF16)
    from_left = dot(pick, left)
    from_right = dot(pick, right)
    column_ref[...] = jnp.where(odd, from_left, from_right).astype(BF16)


def extended(values, up, down, side, links_ref):
    left, right = strips(values.astype(F32), up.astype(F32), down.astype(F32))
    r = iota((EXT, CH), 0) // WIDE
    c = iota((EXT, CH), 0) % WIDE
    spread_row = iota((EXT, WIDE), 0) // WIDE
    spread = (spread_row == iota((EXT, WIDE), 1)).astype(F32).astype(BF16)
    side_rows = dot(spread, side)

    def gate(t, first, middle, last):
        def on(k):
            return (links_ref[0, t, k] >= 0).astype(jnp.int32)

        level = jnp.where(r == 0, on(first), jnp.where(r == WIDE - 1, on(last), on(middle)))
        return level > 0

    out = []
    for t, own, other in ((0, left, right), (1, right, left)):
        keep = jnp.where(r == 0, (links_ref[0, t, 0] >= 0).astype(jnp.int32), 1)
        keep = jnp.where(r == WIDE - 1, (links_ref[0, t, 1] >= 0).astype(jnp.int32), keep)
        centre = pltpu.roll(jnp.where(keep > 0, own, 0.0), 1, 0)
        at_left = side_rows if t == 0 else pltpu.roll(other, EXT - (SIDE - 1), 0)
        at_right = pltpu.roll(other, WIDE - 1, 0) if t == 0 else side_rows
        value = jnp.where(c == 0, jnp.where(gate(t, 4, 2, 6), at_left, 0.0), centre)
        value = jnp.where(c == WIDE - 1, jnp.where(gate(t, 5, 3, 7), at_right, 0.0), value)
        out.append(value)
    return out


def shifted(tiles):
    moved = []
    for b in range(3):
        moved.append([(t if b == 0 else pltpu.roll(t, EXT - b, 0)).astype(BF16) for t in tiles])
    return moved


def window(moved, a, b):
    return jnp.concatenate([t[a * WIDE : a * WIDE + TILE_ROWS] for t in moved[b]], axis=0)


def reduce_kernel(act_ref, w_ref, values_ref, top_ref, bottom_ref, wide):
    wide[...] = jnp.zeros_like(wide)
    wide[:, :, :SIDE, :] = act_ref[0]
    values = dot(wide[...].reshape(ROWS, CH), w_ref[...]).astype(BF16)
    values_ref[...] = values
    rims_of(values, top_ref, bottom_ref)


def spread_taps(group_ref, dense_ref):
    same = iota((CH, CH), 0) // 8 == iota((CH, CH), 1) // 8
    for tap in range(9):
        taps = group_ref[tap // 3, tap % 3].astype(F32)
        full = jnp.concatenate([taps] * (CH // 8), axis=0)
        dense_ref[tap] = jnp.where(same, full, 0.0).astype(BF16)


def prepare_kernel(
    tissue_ref, group_ref, cot_ref, expand_ref, gain_ref, bias_ref,
    scale_ref, mask_ref, dense_ref, out_grad_ref, hidden_grad_ref, wide,
):
    scale_ref[0:1] = gain_ref[...]
    scale_ref[1:2] = bias_ref[...]
    row = iota((TILE_ROWS, SIDE), 0) // WIDE
    pick = (row == iota((TILE_ROWS, SIDE), 1)).astype(F32).astype(BF16)
    col = iota((TILE_ROWS, SIDE), 0) % WIDE
    here = col == iota((TILE_ROWS, SIDE), 1)
    ones = jnp.ones((SIDE, 128), BF16)
    masks = []
    for t in range(2):
        rows = dot(pick, tissue_ref[0, t].astype(F32).astype(BF16))
        masks.append(dot(jnp.where(here, rows, 0.0).astype(BF16), ones))
    mask = jnp.concatenate(masks, axis=0)
    mask_ref[...] = mask
    spread_taps(group_ref, dense_ref)
    wide[...] = jnp.zeros_like(wide)
    wide[:, :, :SIDE, :] = cot_ref[0]
    keep = jnp.concatenate([mask] * (OUT // 128), axis=1) > 0
    out_grad = jnp.where(keep, wide[...].reshape(ROWS, OUT).astype(F32), 0.0).astype(BF16)
    out_grad_ref[...] = out_grad
    hidden_grad_ref[...] = dot(out_grad, expand_ref[...], ((1,), (1,)))


def both(mask):
    return jnp.concatenate([mask, mask], axis=1)


def conv_kernel(
    links_ref, values_ref, up_ref, down_ref, side_ref, dense_ref, mask_ref, hidden_grad_ref,
    joint_ref, padded_ref, sums_ref, top_ref, bottom_ref,
):
    tiles = extended(values_ref[...], up_ref[...], down_ref[...], side_ref[...], links_ref)
    for t in range(2):
        padded_ref[t] = tiles[t].astype(BF16)
    moved = shifted(tiles)
    pre = jnp.zeros((ROWS, CH), F32)
    for a in range(3):
        for b in range(3):
            pre += dot(window(moved, a, b), dense_ref[3 * a + b])
    mask = mask_ref[...]
    joint = jnp.concatenate([pre, hidden_grad_ref[...], mask], axis=1)
    joint_ref[...] = joint
    rims_of(joint, top_ref, bottom_ref)
    held = pre * both(mask)
    block = jnp.concatenate(
        [
            jnp.sum(held, axis=0, keepdims=True),
            jnp.sum(held * pre, axis=0, keepdims=True),
            jnp.sum(mask, axis=0, keepdims=True),
        ],
        axis=1,
    )
    sums_ref[...] = jnp.broadcast_to(block[None], sums_ref.shape)


def between_rims_kernel(
    odd_ref, parts_ref, joint_ref, up_ref, down_ref,
    sums_ref, column_ref,
):
    between_kernel(parts_ref, sums_ref)
    odd = odd_ref[0] == 1
    in_rim = jnp.where(odd, 0, WIDE + SIDE - 1)
    start = jnp.where(odd, 0, TILE_ROWS + SIDE - 1)
    column_ref[0:1] = up_ref[pl.ds(in_rim, 1)]
    column_ref[WIDE - 1 : WIDE] = down_ref[pl.ds(in_rim, 1)]
    for r in range(SIDE):
        column_ref[r + 1 : r + 2] = joint_ref[pl.ds(start + r * WIDE, 1)]


def between_kernel(parts_ref, sums_ref):
    block = jnp.sum(parts_ref[...], axis=0)
    sums_ref[...] = jnp.broadcast_to(block[None], sums_ref.shape)


def moments(parts_ref):
    block = jnp.sum(parts_ref[...], axis=0)
    counted = both(block[:, 2 * CH :])
    centre = block[:, :CH] / counted
    spread = block[:, CH : 2 * CH] / counted - centre * centre
    return centre, lax.rsqrt(spread + EPS), counted


def activated(normed, scale_ref):
    before = scale_ref[0:1] * normed + scale_ref[1:2]
    return before, jax.nn.sigmoid(before)


def through_silu(hidden_grad, before, sigma):
    return hidden_grad * sigma * (1.0 + before * (1.0 - sigma))


def head_kernel(
    parts_ref, joint_ref, scale_ref, out_grad_ref, after_ref, expand_grad_ref, sums_ref,
):
    del after_ref
    centre, inverse, _ = moments(parts_ref)
    normed = (joint_ref[:, :CH] - centre) * inverse
    before, sigma = activated(normed, scale_ref)
    hidden = (before * sigma).astype(BF16)
    expand_grad = dot(hidden, out_grad_ref[...], ((0,), (0,))).astype(BF16)
    expand_grad_ref[:CH] = expand_grad[:, :CH]
    expand_grad_ref[CH:] = expand_grad[:, CH:]
    before_grad = through_silu(joint_ref[:, CH : 2 * CH], before, sigma)
    gain_grad = jnp.sum(before_grad * normed, axis=0, keepdims=True)
    bias_grad = jnp.sum(before_grad, axis=0, keepdims=True)
    block = jnp.concatenate([gain_grad, bias_grad], axis=1)
    sums_ref[...] = jnp.broadcast_to(block[None], sums_ref.shape)


def back_kernel(
    links_ref, parts_ref, totals_ref, joint_ref, scale_ref,
    up_ref, down_ref, side_ref, group_ref, padded_ref, act_ref, w_ref, expand_grad_ref,
    input_grad_ref, packed_ref, gain_grad_ref, bias_grad_ref, wide, dense_ref,
):
    spread_taps(group_ref, dense_ref)
    wide[...] = jnp.zeros_like(wide)
    wide[:, :, :SIDE, :] = act_ref[0]
    act = wide[...].reshape(ROWS, CH)
    centre, inverse, counted = moments(parts_ref)
    totals = jnp.sum(totals_ref[...], axis=0)
    gain_grad = totals[:, :CH]
    bias_grad = totals[:, CH:]
    gain_grad_ref[...] = gain_grad
    bias_grad_ref[...] = bias_grad

    def norm_grad(ref):
        normed = (ref[:, :CH] - centre) * inverse
        before, sigma = activated(normed, scale_ref)
        before_grad = through_silu(ref[:, CH : 2 * CH], before, sigma)
        taken = both(ref[:, 2 * CH :]) * (bias_grad + normed * gain_grad) / counted
        return (scale_ref[0:1] * inverse * (before_grad - taken)).astype(BF16)

    grad, up, down, side = (norm_grad(ref) for ref in (joint_ref, up_ref, down_ref, side_ref))
    moved = shifted(extended(grad, up, down, side, links_ref))
    reduced = jnp.zeros((ROWS, CH), F32)
    for a in range(3):
        for b in range(3):
            reduced += dot(window(moved, a, b), dense_ref[8 - 3 * a - b], ((1,), (1,)))
    in_tile = iota((ROWS, CH), 0) % WIDE < SIDE
    reduced = jnp.where(in_tile, reduced, 0.0).astype(BF16)
    input_grad = dot(reduced, w_ref[...], ((1,), (1,))).astype(BF16)
    input_grad_ref[0] = input_grad.reshape(2, SIDE, WIDE, CH)[:, :, :SIDE, :]
    reduce_grad = dot(act, reduced, ((0,), (0,))).astype(BF16)
    packed_ref[:CH] = reduce_grad
    packed_ref[CH : 3 * CH] = expand_grad_ref[...]
    lowered = []
    for a in range(3):
        parts = []
        for t in range(2):
            own = grad[t * TILE_ROWS : (t + 1) * TILE_ROWS]
            if a:
                parts.append(jnp.zeros((a * WIDE, CH), BF16))
            parts.append(own)
            if a < 2:
                parts.append(jnp.zeros(((2 - a) * WIDE, CH), BF16))
        lowered.append(jnp.concatenate(parts, axis=0))
    lowered = jnp.concatenate(lowered, axis=1)
    windows = shifted([padded_ref[t].astype(F32) for t in range(2)])
    same = iota((CH, CH), 0) // 8 == iota((CH, CH), 1) // 8
    taps = [None] * 9
    for b in range(3):
        product = dot(jnp.concatenate(windows[b], axis=0), lowered, ((0,), (0,)))
        for a in range(3):
            own = jnp.where(same, product[:, a * CH : (a + 1) * CH], 0.0)
            taps[3 * a + b] = jnp.sum(own.reshape(CH // 8, 8, CH), axis=0)
    group = jnp.concatenate(taps + [jnp.zeros((CH - 72, CH), F32)], axis=0).astype(BF16)
    packed_ref[3 * CH :] = group


def total_kernel(parts_ref, total_ref):
    rows = parts_ref.shape[0]
    own = total_ref.shape[1]
    pick = iota((own, rows), 1) % own == iota((own, rows), 0)
    total = dot(pick.astype(F32).astype(BF16), parts_ref[...]).astype(BF16)
    total_ref[...] = jnp.broadcast_to(total[None], total_ref.shape)


def unpack_kernel(packed_ref, reduce_ref, group_ref, expand_ref):
    packed = packed_ref[...].astype(F32)
    reduce_ref[...] = packed[:CH]
    expand_ref[:, :CH] = packed[CH : 2 * CH]
    expand_ref[:, CH:] = packed[2 * CH : 3 * CH]
    group_ref[...] = packed[3 * CH : 3 * CH + 72]


def body(
    sizes, activations, tissue, neighbours, w_reduce, w_group, norm_gain, norm_bias, w_expand,
    cotangent,
):
    dp, long, near = sizes
    space = long * near
    odd = (lax.axis_index(SPACE) % 2).astype(jnp.int32).reshape(1)
    rim = shape((2 * WIDE, CH), BF16)
    flat = shape((ROWS, CH), BF16)
    full = shape((ROWS, CH), F32)

    def rows_passed(top, bottom):
        up = lax.ppermute(bottom, SPACE, [(i, i + 2) for i in range(space - 2)])
        down = lax.ppermute(top, SPACE, [(i + 2, i) for i in range(space - 2)])
        return up, down

    def column_passed(column):
        return lax.ppermute(column, SPACE, [(i, i ^ 1) for i in range(space)])

    values, top, bottom = call(
        reduce_kernel, (flat, rim, rim), [VMEM] * 2, [pltpu.VMEM((2, SIDE, WIDE, CH), BF16)]
    )(activations, w_reduce)
    scale, mask, dense, out_grad, hidden_grad = call(
        prepare_kernel,
        (
            shape((2, CH), F32),
            shape((ROWS, 128), F32),
            shape((9, CH, CH), BF16),
            shape((ROWS, OUT), BF16),
            full,
        ),
        [VMEM] * 6,
        [pltpu.VMEM((2, SIDE, WIDE, OUT), BF16)],
    )(
        tissue, w_group, cotangent, w_expand, norm_gain.reshape(1, CH), norm_bias.reshape(1, CH)
    )
    up, down = rows_passed(top, bottom)
    column = call(
        column_kernel, shape((WIDE, CH), BF16), [SMEM] + [VMEM] * 3 + [HBM]
    )(odd, values, up, down, mask)
    side = column_passed(column)

    width = 2 * CH + 128
    rim = shape((2 * WIDE, width), F32)
    joint, padded, sums, top, bottom = call(
        conv_kernel,
        (
            shape((ROWS, width), F32),
            shape((2, EXT, CH), BF16),
            shape((near, 1, width), F32),
            rim,
            rim,
        ),
        [SMEM] + [VMEM] * 7,
    )(neighbours, values, up, down, side, dense, mask, hidden_grad)
    up, down = rows_passed(top, bottom)
    parts = lax.all_to_all(sums, "near", 0, 0)
    sums, column = call(
        between_rims_kernel,
        (shape((dp * long, 1, width), F32), shape((WIDE, width), F32)),
        [SMEM] + [VMEM] * 4,
    )(odd, parts, joint, up, down)
    side = column_passed(column)
    parts = lax.all_to_all(sums, FAR, 0, 0)

    expand_grad, sums = call(
        head_kernel,
        (shape((2 * CH, CH), BF16), shape((near, 1, 2 * CH), F32)),
        [VMEM] * 4 + [HBM],
    )(parts, joint, scale, out_grad, side)
    totals = lax.all_to_all(sums, "near", 0, 0)
    sums = call(between_kernel, shape((dp * long, 1, 2 * CH), F32), [VMEM])(totals)
    totals = lax.all_to_all(sums, FAR, 0, 0)

    input_grad, packed, gain_grad, bias_grad = call(
        back_kernel,
        (
            shape((1, 2, SIDE, SIDE, CH), BF16),
            shape((4 * CH, CH), BF16),
            shape((1, CH), F32),
            shape((1, CH), F32),
        ),
        [SMEM] + [VMEM] * 12,
        [pltpu.VMEM((2, SIDE, WIDE, CH), BF16), pltpu.VMEM((9, CH, CH), BF16)],
    )(
        neighbours, parts, totals, joint, scale, up, down, side, w_group, padded,
        activations, w_reduce, expand_grad,
    )
    count = dp * space
    shares = (count, packed.shape[0] // count, CH)
    received = lax.all_to_all(packed.reshape(shares), ALL, 0, 0)
    total = call(total_kernel, shape(shares, BF16), [VMEM])(received.reshape(packed.shape))
    gathered = lax.all_to_all(total, ALL, 0, 0)
    reduce_grad, group_grad, expand_grad = call(
        unpack_kernel,
        (shape((CH, CH), F32), shape((72, CH), F32), shape((CH, OUT), F32)),
        [VMEM],
    )(gathered.reshape(packed.shape))
    return (
        input_grad,
        reduce_grad,
        group_grad.reshape(3, 3, 8, CH),
        gain_grad.reshape(CH),
        bias_grad.reshape(CH),
        expand_grad,
    )


def solution(mesh):
    dp = mesh.shape["dp"]
    near = min(16, mesh.shape["space"])
    long = mesh.shape["space"] // near
    cut = Mesh(mesh.devices.reshape(dp, long, near), ("dp", "long", "near"))
    return jax.shard_map(
        functools.partial(body, (dp, long, near)),
        mesh=cut,
        in_specs=(
            P("dp", SPACE, None, None, None),
            P("dp", SPACE, None, None),
            P("dp", SPACE, None),
            P(),
            P(),
            P(),
            P(),
            P(),
            P("dp", SPACE, None, None, None),
        ),
        out_specs=(P("dp", SPACE, None, None, None), P(), P(), P(), P(), P()),
        check_vma=False,
    )
```

```python
import functools

import jax
import jax.numpy as jnp
from jax import lax
from jax.experimental import pallas as pl
from jax.experimental.pallas import tpu as pltpu
from jax.sharding import Mesh
from jax.sharding import PartitionSpec as P

SPACE = ("long", "near")
FAR = ("dp", "long")
ALL = ("dp", "long", "near")
EPS = 1e-05
SIDE = 14
WIDE = 16
TILE_ROWS = SIDE * WIDE
ROWS = 2 * TILE_ROWS
EXT = WIDE * WIDE
CH = 256
OUT = 512
F32 = jnp.float32
BF16 = jnp.bfloat16

VMEM = pl.BlockSpec(memory_space=pltpu.VMEM)
SMEM = pl.BlockSpec(memory_space=pltpu.SMEM)
HBM = pl.BlockSpec(memory_space=pl.ANY)
PARAMS = pltpu.CompilerParams(vmem_limit_bytes=24 * 1024 * 1024)


def call(kernel, outs, specs, scratch=()):
    return pl.pallas_call(
        kernel,
        out_shape=outs,
        in_specs=specs,
        out_specs=jax.tree.map(lambda _: VMEM, outs),
        scratch_shapes=scratch,
        compiler_params=PARAMS,
    )


def shape(dims, kind):
    return jax.ShapeDtypeStruct(dims, kind)


def dot(a, b, dims=((1,), (0,))):
    return lax.dot_general(a, b, (dims, ((), ())), preferred_element_type=F32)


def iota(dims, axis):
    return lax.broadcasted_iota(jnp.int32, dims, axis)


def rims_of(values, top_ref, bottom_ref):
    for t in range(2):
        first = t * TILE_ROWS
        last = first + TILE_ROWS - WIDE
        top_ref[t * WIDE : (t + 1) * WIDE] = values[first : first + WIDE]
        bottom_ref[t * WIDE : (t + 1) * WIDE] = values[last : last + WIDE]


def strips(values, up, down):
    out = []
    for t in range(2):
        out.append(
            jnp.concatenate(
                [
                    up[t * WIDE : (t + 1) * WIDE],
                    values[t * TILE_ROWS : (t + 1) * TILE_ROWS],
                    down[t * WIDE : (t + 1) * WIDE],
                ],
                axis=0,
            )
        )
    return out


def column_kernel(odd_ref, values_ref, up_ref, down_ref, after_ref, column_ref):
    del after_ref
    left, right = strips(values_ref[...], up_ref[...], down_ref[...])
    row = iota((WIDE, EXT), 0)
    place = iota((WIDE, EXT), 1)
    odd = odd_ref[0] == 1
    wanted = row * WIDE + jnp.where(odd, 0, SIDE - 1)
    pick = (place == wanted).astype(F32).astype(BF16)
    from_left = dot(pick, left)
    from_right = dot(pick, right)
    column_ref[...] = jnp.where(odd, from_left, from_right).astype(BF16)


def extended(values, up, down, side, links_ref):
    left, right = strips(values.astype(F32), up.astype(F32), down.astype(F32))
    r = iota((EXT, CH), 0) // WIDE
    c = iota((EXT, CH), 0) % WIDE
    spread_row = iota((EXT, WIDE), 0) // WIDE
    spread = (spread_row == iota((EXT, WIDE), 1)).astype(F32).astype(BF16)
    side_rows = dot(spread, side)

    def gate(t, first, middle, last):
        def on(k):
            return (links_ref[0, t, k] >= 0).astype(jnp.int32)

        level = jnp.where(r == 0, on(first), jnp.where(r == WIDE - 1, on(last), on(middle)))
        return level > 0

    out = []
    for t, own, other in ((0, left, right), (1, right, left)):
        keep = jnp.where(r == 0, (links_ref[0, t, 0] >= 0).astype(jnp.int32), 1)
        keep = jnp.where(r == WIDE - 1, (links_ref[0, t, 1] >= 0).astype(jnp.int32), keep)
        centre = pltpu.roll(jnp.where(keep > 0, own, 0.0), 1, 0)
        at_left = side_rows if t == 0 else pltpu.roll(other, EXT - (SIDE - 1), 0)
        at_right = pltpu.roll(other, WIDE - 1, 0) if t == 0 else side_rows
        value = jnp.where(c == 0, jnp.where(gate(t, 4, 2, 6), at_left, 0.0), centre)
        value = jnp.where(c == WIDE - 1, jnp.where(gate(t, 5, 3, 7), at_right, 0.0), value)
        out.append(value)
    return out


def shifted(tiles):
    moved = []
    for b in range(3):
        moved.append([(t if b == 0 else pltpu.roll(t, EXT - b, 0)).astype(BF16) for t in tiles])
    return moved


def window(moved, a, b):
    return jnp.concatenate([t[a * WIDE : a * WIDE + TILE_ROWS] for t in moved[b]], axis=0)


def reduce_kernel(act_ref, w_ref, values_ref, top_ref, bottom_ref, wide):
    wide[...] = jnp.zeros_like(wide)
    wide[:, :, :SIDE, :] = act_ref[0]
    values = dot(wide[...].reshape(ROWS, CH), w_ref[...]).astype(BF16)
    values_ref[...] = values
    rims_of(values, top_ref, bottom_ref)


def spread_taps(group_ref, dense_ref):
    same = iota((CH, CH), 0) // 8 == iota((CH, CH), 1) // 8
    for tap in range(9):
        taps = group_ref[tap // 3, tap % 3].astype(F32)
        full = jnp.concatenate([taps] * (CH // 8), axis=0)
        dense_ref[tap] = jnp.where(same, full, 0.0).astype(BF16)


def prepare_kernel(
    tissue_ref, group_ref, cot_ref, expand_ref, gain_ref, bias_ref,
    scale_ref, mask_ref, dense_ref, out_grad_ref, hidden_grad_ref, wide,
):
    scale_ref[0:1] = gain_ref[...]
    scale_ref[1:2] = bias_ref[...]
    row = iota((TILE_ROWS, SIDE), 0) // WIDE
    pick = (row == iota((TILE_ROWS, SIDE), 1)).astype(F32).astype(BF16)
    col = iota((TILE_ROWS, SIDE), 0) % WIDE
    here = col == iota((TILE_ROWS, SIDE), 1)
    ones = jnp.ones((SIDE, 128), BF16)
    masks = []
    for t in range(2):
        rows = dot(pick, tissue_ref[0, t].astype(F32).astype(BF16))
        masks.append(dot(jnp.where(here, rows, 0.0).astype(BF16), ones))
    mask = jnp.concatenate(masks, axis=0)
    mask_ref[...] = mask
    spread_taps(group_ref, dense_ref)
    wide[...] = jnp.zeros_like(wide)
    wide[:, :, :SIDE, :] = cot_ref[0]
    keep = jnp.concatenate([mask] * (OUT // 128), axis=1) > 0
    out_grad = jnp.where(keep, wide[...].reshape(ROWS, OUT).astype(F32), 0.0).astype(BF16)
    out_grad_ref[...] = out_grad
    hidden_grad_ref[...] = dot(out_grad, expand_ref[...], ((1,), (1,)))


def both(mask):
    return jnp.concatenate([mask, mask], axis=1)


def conv_kernel(
    links_ref, values_ref, up_ref, down_ref, side_ref, dense_ref, mask_ref, hidden_grad_ref,
    joint_ref, padded_ref, sums_ref,
):
    tiles = extended(values_ref[...], up_ref[...], down_ref[...], side_ref[...], links_ref)
    for t in range(2):
        padded_ref[t] = tiles[t].astype(BF16)
    moved = shifted(tiles)
    pre = jnp.zeros((ROWS, CH), F32)
    for a in range(3):
        for b in range(3):
            pre += dot(window(moved, a, b), dense_ref[3 * a + b])
    mask = mask_ref[...]
    joint = jnp.concatenate([pre, hidden_grad_ref[...], mask], axis=1)
    joint_ref[...] = joint
    held = pre * both(mask)
    block = jnp.concatenate(
        [
            jnp.sum(held, axis=0, keepdims=True),
            jnp.sum(held * pre, axis=0, keepdims=True),
            jnp.sum(mask, axis=0, keepdims=True),
        ],
        axis=1,
    )
    sums_ref[...] = jnp.broadcast_to(block[None], sums_ref.shape)


def between_rows_kernel(parts_ref, joint_ref, sums_ref, top_ref, bottom_ref):
    between_kernel(parts_ref, sums_ref)
    rims_of(joint_ref, top_ref, bottom_ref)


def between_column_kernel(
    odd_ref, parts_ref, joint_ref, up_ref, down_ref, sums_ref, column_ref
):
    between_kernel(parts_ref, sums_ref)
    odd = odd_ref[0] == 1
    in_rim = jnp.where(odd, 0, WIDE + SIDE - 1)
    start = jnp.where(odd, 0, TILE_ROWS + SIDE - 1)
    column_ref[0:1] = up_ref[pl.ds(in_rim, 1)]
    column_ref[WIDE - 1 : WIDE] = down_ref[pl.ds(in_rim, 1)]
    for r in range(SIDE):
        column_ref[r + 1 : r + 2] = joint_ref[pl.ds(start + r * WIDE, 1)]


def between_kernel(parts_ref, sums_ref):
    block = jnp.sum(parts_ref[...], axis=0)
    sums_ref[...] = jnp.broadcast_to(block[None], sums_ref.shape)


def moments(parts_ref):
    block = jnp.sum(parts_ref[...], axis=0)
    counted = both(block[:, 2 * CH :])
    centre = block[:, :CH] / counted
    spread = block[:, CH : 2 * CH] / counted - centre * centre
    return centre, lax.rsqrt(spread + EPS), counted


def activated(normed, scale_ref):
    before = scale_ref[0:1] * normed + scale_ref[1:2]
    return before, jax.nn.sigmoid(before)


def through_silu(hidden_grad, before, sigma):
    return hidden_grad * sigma * (1.0 + before * (1.0 - sigma))


def head_kernel(
    parts_ref, joint_ref, scale_ref, out_grad_ref, expand_grad_ref, sums_ref,
):
    centre, inverse, _ = moments(parts_ref)
    normed = (joint_ref[:, :CH] - centre) * inverse
    before, sigma = activated(normed, scale_ref)
    hidden = (before * sigma).astype(BF16)
    expand_grad = dot(hidden, out_grad_ref[...], ((0,), (0,))).astype(BF16)
    expand_grad_ref[:CH] = expand_grad[:, :CH]
    expand_grad_ref[CH:] = expand_grad[:, CH:]
    before_grad = through_silu(joint_ref[:, CH : 2 * CH], before, sigma)
    gain_grad = jnp.sum(before_grad * normed, axis=0, keepdims=True)
    bias_grad = jnp.sum(before_grad, axis=0, keepdims=True)
    block = jnp.concatenate([gain_grad, bias_grad], axis=1)
    sums_ref[...] = jnp.broadcast_to(block[None], sums_ref.shape)


def back_kernel(
    links_ref, parts_ref, totals_ref, joint_ref, scale_ref,
    up_ref, down_ref, side_ref, group_ref, padded_ref, act_ref, w_ref, expand_grad_ref,
    input_grad_ref, packed_ref, gain_grad_ref, bias_grad_ref, wide, dense_ref,
):
    spread_taps(group_ref, dense_ref)
    wide[...] = jnp.zeros_like(wide)
    wide[:, :, :SIDE, :] = act_ref[0]
    act = wide[...].reshape(ROWS, CH)
    centre, inverse, counted = moments(parts_ref)
    totals = jnp.sum(totals_ref[...], axis=0)
    gain_grad = totals[:, :CH]
    bias_grad = totals[:, CH:]
    gain_grad_ref[...] = gain_grad
    bias_grad_ref[...] = bias_grad

    def norm_grad(ref):
        normed = (ref[:, :CH] - centre) * inverse
        before, sigma = activated(normed, scale_ref)
        before_grad = through_silu(ref[:, CH : 2 * CH], before, sigma)
        taken = both(ref[:, 2 * CH :]) * (bias_grad + normed * gain_grad) / counted
        return (scale_ref[0:1] * inverse * (before_grad - taken)).astype(BF16)

    grad, up, down, side = (norm_grad(ref) for ref in (joint_ref, up_ref, down_ref, side_ref))
    moved = shifted(extended(grad, up, down, side, links_ref))
    reduced = jnp.zeros((ROWS, CH), F32)
    for a in range(3):
        for b in range(3):
            reduced += dot(window(moved, a, b), dense_ref[8 - 3 * a - b], ((1,), (1,)))
    in_tile = iota((ROWS, CH), 0) % WIDE < SIDE
    reduced = jnp.where(in_tile, reduced, 0.0).astype(BF16)
    input_grad = dot(reduced, w_ref[...], ((1,), (1,))).astype(BF16)
    input_grad_ref[0] = input_grad.reshape(2, SIDE, WIDE, CH)[:, :, :SIDE, :]
    reduce_grad = dot(act, reduced, ((0,), (0,))).astype(BF16)
    packed_ref[:CH] = reduce_grad
    packed_ref[CH : 3 * CH] = expand_grad_ref[...]
    tall = [grad[t * TILE_ROWS : (t + 1) * TILE_ROWS].astype(F32) for t in range(2)]
    tall = [jnp.concatenate([own, jnp.zeros((2 * WIDE, CH), F32)], axis=0) for own in tall]
    aside = [[(pltpu.roll(own, b, 0) if b else own).astype(BF16) for own in tall] for b in range(3)]
    lowered = []
    for a in range(3):
        for b in range(3):
            parts = []
            for t in range(2):
                if a:
                    parts.append(jnp.zeros((a * WIDE, CH), BF16))
                parts.append(aside[b][t][: EXT - a * WIDE])
            lowered.append(jnp.concatenate(parts, axis=0))
    padded = jnp.concatenate([padded_ref[0], padded_ref[1]], axis=0)
    same = iota((128, 128), 0) // 8 == iota((128, 128), 1) // 8
    halves = []
    for h in range(2):
        lanes = slice(h * 128, (h + 1) * 128)
        right = jnp.concatenate([x[:, lanes] for x in lowered], axis=1)
        product = dot(padded[:, lanes], right, ((0,), (0,)))
        taps = []
        for k in range(9):
            own = jnp.where(same, product[:, k * 128 : (k + 1) * 128], 0.0)
            taps.append(jnp.sum(own.reshape(128 // 8, 8, 128), axis=0))
        halves.append(jnp.concatenate(taps, axis=0))
    taps = [jnp.concatenate(halves, axis=1)]
    group = jnp.concatenate(taps + [jnp.zeros((CH - 72, CH), F32)], axis=0).astype(BF16)
    packed_ref[3 * CH :] = group


def total_kernel(parts_ref, total_ref):
    rows = parts_ref.shape[0]
    own = total_ref.shape[1]
    pick = iota((own, rows), 1) % own == iota((own, rows), 0)
    total = dot(pick.astype(F32).astype(BF16), parts_ref[...]).astype(BF16)
    total_ref[...] = jnp.broadcast_to(total[None], total_ref.shape)


def unpack_kernel(packed_ref, reduce_ref, group_ref, expand_ref):
    packed = packed_ref[...].astype(F32)
    reduce_ref[...] = packed[:CH]
    expand_ref[:, :CH] = packed[CH : 2 * CH]
    expand_ref[:, CH:] = packed[2 * CH : 3 * CH]
    group_ref[...] = packed[3 * CH : 3 * CH + 72]


def body(
    sizes, activations, tissue, neighbours, w_reduce, w_group, norm_gain, norm_bias, w_expand,
    cotangent,
):
    dp, long, near = sizes
    space = long * near
    odd = (lax.axis_index(SPACE) % 2).astype(jnp.int32).reshape(1)
    rim = shape((2 * WIDE, CH), BF16)
    flat = shape((ROWS, CH), BF16)
    full = shape((ROWS, CH), F32)

    def rows_passed(top, bottom):
        up = lax.ppermute(bottom, SPACE, [(i, i + 2) for i in range(space - 2)])
        down = lax.ppermute(top, SPACE, [(i + 2, i) for i in range(space - 2)])
        return up, down

    def column_passed(column):
        return lax.ppermute(column, SPACE, [(i, i ^ 1) for i in range(space)])

    values, top, bottom = call(
        reduce_kernel, (flat, rim, rim), [VMEM] * 2, [pltpu.VMEM((2, SIDE, WIDE, CH), BF16)]
    )(activations, w_reduce)
    scale, mask, dense, out_grad, hidden_grad = call(
        prepare_kernel,
        (
            shape((2, CH), F32),
            shape((ROWS, 128), F32),
            shape((9, CH, CH), BF16),
            shape((ROWS, OUT), BF16),
            full,
        ),
        [VMEM] * 6,
        [pltpu.VMEM((2, SIDE, WIDE, OUT), BF16)],
    )(
        tissue, w_group, cotangent, w_expand, norm_gain.reshape(1, CH), norm_bias.reshape(1, CH)
    )
    up, down = rows_passed(top, bottom)
    column = call(
        column_kernel, shape((WIDE, CH), BF16), [SMEM] + [VMEM] * 3 + [HBM]
    )(odd, values, up, down, mask)
    side = column_passed(column)

    width = 2 * CH + 128
    rim = shape((2 * WIDE, width), F32)
    joint, padded, sums = call(
        conv_kernel,
        (
            shape((ROWS, width), F32),
            shape((2, EXT, CH), BF16),
            shape((near, 1, width), F32),
        ),
        [SMEM] + [VMEM] * 7,
    )(neighbours, values, up, down, side, dense, mask, hidden_grad)
    parts = lax.all_to_all(sums, "near", 0, 0)
    sums, top, bottom = call(
        between_rows_kernel, (shape((dp * long, 1, width), F32), rim, rim), [VMEM] * 2
    )(parts, joint)
    up, down = rows_passed(top, bottom)
    parts = lax.all_to_all(sums, FAR, 0, 0)

    expand_grad, sums = call(
        head_kernel,
        (shape((2 * CH, CH), BF16), shape((near, 1, 2 * CH), F32)),
        [VMEM] * 4,
    )(parts, joint, scale, out_grad)
    totals = lax.all_to_all(sums, "near", 0, 0)
    sums, column = call(
        between_column_kernel,
        (shape((dp * long, 1, 2 * CH), F32), shape((WIDE, width), F32)),
        [SMEM] + [VMEM] * 4,
    )(odd, totals, joint, up, down)
    side = column_passed(column)
    totals = lax.all_to_all(sums, FAR, 0, 0)

    input_grad, packed, gain_grad, bias_grad = call(
        back_kernel,
        (
            shape((1, 2, SIDE, SIDE, CH), BF16),
            shape((4 * CH, CH), BF16),
            shape((1, CH), F32),
            shape((1, CH), F32),
        ),
        [SMEM] + [VMEM] * 12,
        [pltpu.VMEM((2, SIDE, WIDE, CH), BF16), pltpu.VMEM((9, CH, CH), BF16)],
    )(
        neighbours, parts, totals, joint, scale, up, down, side, w_group, padded,
        activations, w_reduce, expand_grad,
    )
    count = dp * space
    shares = (count, packed.shape[0] // count, CH)
    received = lax.all_to_all(packed.reshape(shares), ALL, 0, 0)
    total = call(total_kernel, shape(shares, BF16), [VMEM])(received.reshape(packed.shape))
    gathered = lax.all_to_all(total, ALL, 0, 0)
    reduce_grad, group_grad, expand_grad = call(
        unpack_kernel,
        (shape((CH, CH), F32), shape((72, CH), F32), shape((CH, OUT), F32)),
        [VMEM],
    )(gathered.reshape(packed.shape))
    return (
        input_grad,
        reduce_grad,
        group_grad.reshape(3, 3, 8, CH),
        gain_grad.reshape(CH),
        bias_grad.reshape(CH),
        expand_grad,
    )


def solution(mesh):
    dp = mesh.shape["dp"]
    near = min(16, mesh.shape["space"])
    long = mesh.shape["space"] // near
    cut = Mesh(mesh.devices.reshape(dp, long, near), ("dp", "long", "near"))
    return jax.shard_map(
        functools.partial(body, (dp, long, near)),
        mesh=cut,
        in_specs=(
            P("dp", SPACE, None, None, None),
            P("dp", SPACE, None, None),
            P("dp", SPACE, None),
            P(),
            P(),
            P(),
            P(),
            P(),
            P("dp", SPACE, None, None, None),
        ),
        out_specs=(P("dp", SPACE, None, None, None), P(), P(), P(), P(), P()),
        check_vma=False,
    )
```

```python
import functools
import math

import jax
import jax.numpy as jnp
from jax import lax
from jax.experimental import pallas as pl
from jax.experimental.pallas import tpu as pltpu
from jax.sharding import Mesh
from jax.sharding import PartitionSpec as P

DP = ("zh", "x")
SPACE = ("zl", "y", "core")
NEAR = ("y", "core")
FAR = ("zh", "x", "zl")
FIRST = ("x", "core")
SECOND = ("zh", "zl", "y")
EPS = 1e-05
SIDE = 14
WIDE = 16
TILE_ROWS = SIDE * WIDE
ROWS = 2 * TILE_ROWS
SPARE = WIDE - 1
EXT = WIDE * WIDE
CH = 256
OUT = 512
F32 = jnp.float32
BF16 = jnp.bfloat16

VMEM = pl.BlockSpec(memory_space=pltpu.VMEM)
SMEM = pl.BlockSpec(memory_space=pltpu.SMEM)
HBM = pl.BlockSpec(memory_space=pl.ANY)
PARAMS = pltpu.CompilerParams(vmem_limit_bytes=24 * 1024 * 1024)


def call(kernel, outs, specs, scratch=()):
    return pl.pallas_call(
        kernel,
        out_shape=outs,
        in_specs=specs,
        out_specs=jax.tree.map(lambda _: VMEM, outs),
        scratch_shapes=scratch,
        compiler_params=PARAMS,
    )


def shape(dims, kind):
    return jax.ShapeDtypeStruct(dims, kind)


def dot(a, b, dims=((1,), (0,))):
    return lax.dot_general(a, b, (dims, ((), ())), preferred_element_type=F32)


def iota(dims, axis):
    return lax.broadcasted_iota(jnp.int32, dims, axis)


def rims_of(values, top_ref, bottom_ref):
    for t in range(2):
        first = t * TILE_ROWS
        last = first + TILE_ROWS - WIDE
        top_ref[t * WIDE : (t + 1) * WIDE] = values[first : first + WIDE]
        bottom_ref[t * WIDE : (t + 1) * WIDE] = values[last : last + WIDE]


def strips(values, up, down):
    out = []
    for t in range(2):
        out.append(
            jnp.concatenate(
                [
                    up[t * WIDE : (t + 1) * WIDE],
                    values[t * TILE_ROWS : (t + 1) * TILE_ROWS],
                    down[t * WIDE : (t + 1) * WIDE],
                ],
                axis=0,
            )
        )
    return out


def extended(values, up, down, side, links_ref):
    left, right = strips(values.astype(F32), up.astype(F32), down.astype(F32))
    r = iota((EXT, CH), 0) // WIDE
    c = iota((EXT, CH), 0) % WIDE
    spread_row = iota((EXT, WIDE), 0) // WIDE
    spread = (spread_row == iota((EXT, WIDE), 1)).astype(F32).astype(BF16)
    side_rows = dot(spread, side)

    def gate(t, first, middle, last):
        def on(k):
            return (links_ref[0, t, k] >= 0).astype(jnp.int32)

        level = jnp.where(r == 0, on(first), jnp.where(r == WIDE - 1, on(last), on(middle)))
        return level > 0

    out = []
    for t, own, other in ((0, left, right), (1, right, left)):
        keep = jnp.where(r == 0, (links_ref[0, t, 0] >= 0).astype(jnp.int32), 1)
        keep = jnp.where(r == WIDE - 1, (links_ref[0, t, 1] >= 0).astype(jnp.int32), keep)
        centre = pltpu.roll(jnp.where(keep > 0, own, 0.0), 1, 0)
        at_left = side_rows if t == 0 else pltpu.roll(other, EXT - (SIDE - 1), 0)
        at_right = pltpu.roll(other, WIDE - 1, 0) if t == 0 else side_rows
        value = jnp.where(c == 0, jnp.where(gate(t, 4, 2, 6), at_left, 0.0), centre)
        value = jnp.where(c == WIDE - 1, jnp.where(gate(t, 5, 3, 7), at_right, 0.0), value)
        out.append(value)
    return out


def shifted(tiles):
    moved = []
    for b in range(3):
        moved.append([(t if b == 0 else pltpu.roll(t, EXT - b, 0)).astype(BF16) for t in tiles])
    return moved


def window(moved, a, b):
    return jnp.concatenate([t[a * WIDE : a * WIDE + TILE_ROWS] for t in moved[b]], axis=0)


def reduce_kernel(
    odd_ref, act_ref, beside_ref, w_ref, values_ref, top_ref, bottom_ref, side_ref, wide
):
    wide[...] = jnp.zeros_like(wide)
    wide[:, :, :SIDE, :] = act_ref[0]
    values = dot(wide[...].reshape(ROWS, CH), w_ref[...]).astype(BF16)
    values_ref[...] = values
    down_one = iota((WIDE, SIDE), 0) == iota((WIDE, SIDE), 1) + 1
    down_one = down_one.astype(F32).astype(BF16)
    pixels = jnp.where(odd_ref[0] == 1, dot(down_one, beside_ref[0]), dot(down_one, beside_ref[1]))
    side = dot(pixels.astype(BF16), w_ref[...])
    side_ref[...] = side.astype(BF16)
    for rim_ref, first, corner in ((top_ref, 0, 1), (bottom_ref, TILE_ROWS - WIDE, SIDE)):
        strip = [values[t * TILE_ROWS + first :][:WIDE].astype(F32) for t in range(2)]
        strip = jnp.concatenate(strip, axis=0)
        spare = iota((2 * WIDE, CH), 0) == SPARE
        rim_ref[...] = jnp.where(spare, side[corner : corner + 1], strip).astype(BF16)


def spread_taps(group_ref, dense_ref):
    same = iota((CH, CH), 0) // 8 == iota((CH, CH), 1) // 8
    for tap in range(9):
        taps = group_ref[tap // 3, tap % 3].astype(F32)
        full = jnp.concatenate([taps] * (CH // 8), axis=0)
        dense_ref[tap] = jnp.where(same, full, 0.0).astype(BF16)


def prepare_kernel(
    tissue_ref, group_ref, cot_ref, expand_ref, gain_ref, bias_ref,
    scale_ref, mask_ref, dense_ref, out_grad_ref, hidden_grad_ref, wide,
):
    scale_ref[0:1] = gain_ref[...]
    scale_ref[1:2] = bias_ref[...]
    row = iota((TILE_ROWS, SIDE), 0) // WIDE
    pick = (row == iota((TILE_ROWS, SIDE), 1)).astype(F32).astype(BF16)
    col = iota((TILE_ROWS, SIDE), 0) % WIDE
    here = col == iota((TILE_ROWS, SIDE), 1)
    ones = jnp.ones((SIDE, 128), BF16)
    masks = []
    for t in range(2):
        rows = dot(pick, tissue_ref[0, t].astype(F32).astype(BF16))
        masks.append(dot(jnp.where(here, rows, 0.0).astype(BF16), ones))
    mask = jnp.concatenate(masks, axis=0)
    mask_ref[...] = mask
    spread_taps(group_ref, dense_ref)
    wide[...] = jnp.zeros_like(wide)
    wide[:, :, :SIDE, :] = cot_ref[0]
    keep = jnp.concatenate([mask] * (OUT // 128), axis=1) > 0
    out_grad = jnp.where(keep, wide[...].reshape(ROWS, OUT).astype(F32), 0.0).astype(BF16)
    out_grad_ref[...] = out_grad
    hidden_grad_ref[...] = dot(out_grad, expand_ref[...], ((1,), (1,)))


def both(mask):
    return jnp.concatenate([mask, mask], axis=1)


def conv_kernel(
    links_ref, values_ref, up_ref, down_ref, side_ref, dense_ref, mask_ref, hidden_grad_ref,
    joint_ref, padded_ref, sums_ref,
):
    up, down, side = up_ref[...], down_ref[...], side_ref[...].astype(F32)
    row = iota((WIDE, CH), 0)
    side = jnp.where(row == 0, up[SPARE : SPARE + 1].astype(F32), side)
    side = jnp.where(row == WIDE - 1, down[SPARE : SPARE + 1].astype(F32), side)
    tiles = extended(values_ref[...], up, down, side.astype(BF16), links_ref)
    for t in range(2):
        padded_ref[t] = tiles[t].astype(BF16)
    moved = shifted(tiles)
    pre = jnp.zeros((ROWS, CH), F32)
    for a in range(3):
        for b in range(3):
            pre += dot(window(moved, a, b), dense_ref[3 * a + b])
    mask = mask_ref[...]
    joint = jnp.concatenate([pre, hidden_grad_ref[...], mask], axis=1)
    joint_ref[...] = joint
    held = pre * both(mask)
    block = jnp.concatenate(
        [
            jnp.sum(held, axis=0, keepdims=True),
            jnp.sum(held * pre, axis=0, keepdims=True),
            jnp.sum(mask, axis=0, keepdims=True),
        ],
        axis=1,
    )
    sums_ref[...] = jnp.broadcast_to(block[None], sums_ref.shape)


def between_rows_kernel(parts_ref, joint_ref, sums_ref, top_ref, bottom_ref):
    between_kernel(parts_ref, sums_ref)
    rims_of(joint_ref, top_ref, bottom_ref)


def between_column_kernel(
    odd_ref, parts_ref, joint_ref, up_ref, down_ref, sums_ref, column_ref
):
    between_kernel(parts_ref, sums_ref)
    odd = odd_ref[0] == 1
    in_rim = jnp.where(odd, 0, WIDE + SIDE - 1)
    start = jnp.where(odd, 0, TILE_ROWS + SIDE - 1)
    column_ref[0:1] = up_ref[pl.ds(in_rim, 1)]
    column_ref[WIDE - 1 : WIDE] = down_ref[pl.ds(in_rim, 1)]
    for r in range(SIDE):
        column_ref[r + 1 : r + 2] = joint_ref[pl.ds(start + r * WIDE, 1)]


def between_kernel(parts_ref, sums_ref):
    block = jnp.sum(parts_ref[...], axis=0)
    sums_ref[...] = jnp.broadcast_to(block[None], sums_ref.shape)


def moments(parts_ref):
    block = jnp.sum(parts_ref[...], axis=0)
    counted = both(block[:, 2 * CH :])
    centre = block[:, :CH] / counted
    spread = block[:, CH : 2 * CH] / counted - centre * centre
    return centre, lax.rsqrt(spread + EPS), counted


def activated(normed, scale_ref):
    before = scale_ref[0:1] * normed + scale_ref[1:2]
    return before, jax.nn.sigmoid(before)


def through_silu(hidden_grad, before, sigma):
    return hidden_grad * sigma * (1.0 + before * (1.0 - sigma))


def head_kernel(
    parts_ref, joint_ref, scale_ref, out_grad_ref, expand_grad_ref, sums_ref,
):
    centre, inverse, _ = moments(parts_ref)
    normed = (joint_ref[:, :CH] - centre) * inverse
    before, sigma = activated(normed, scale_ref)
    hidden = (before * sigma).astype(BF16)
    expand_grad = dot(hidden, out_grad_ref[...], ((0,), (0,))).astype(BF16)
    expand_grad_ref[:CH] = expand_grad[:, :CH]
    expand_grad_ref[CH:] = expand_grad[:, CH:]
    before_grad = through_silu(joint_ref[:, CH : 2 * CH], before, sigma)
    gain_grad = jnp.sum(before_grad * normed, axis=0, keepdims=True)
    bias_grad = jnp.sum(before_grad, axis=0, keepdims=True)
    block = jnp.concatenate([gain_grad, bias_grad], axis=1)
    sums_ref[...] = jnp.broadcast_to(block[None], sums_ref.shape)


def back_kernel(
    links_ref, parts_ref, totals_ref, joint_ref, scale_ref,
    up_ref, down_ref, side_ref, group_ref, padded_ref, act_ref, w_ref, expand_grad_ref,
    input_grad_ref, packed_ref, gain_grad_ref, bias_grad_ref, wide, dense_ref,
):
    spread_taps(group_ref, dense_ref)
    wide[...] = jnp.zeros_like(wide)
    wide[:, :, :SIDE, :] = act_ref[0]
    act = wide[...].reshape(ROWS, CH)
    centre, inverse, counted = moments(parts_ref)
    totals = jnp.sum(totals_ref[...], axis=0)
    gain_grad = totals[:, :CH]
    bias_grad = totals[:, CH:]
    gain_grad_ref[...] = gain_grad
    bias_grad_ref[...] = bias_grad

    def norm_grad(ref):
        normed = (ref[:, :CH] - centre) * inverse
        before, sigma = activated(normed, scale_ref)
        before_grad = through_silu(ref[:, CH : 2 * CH], before, sigma)
        taken = both(ref[:, 2 * CH :]) * (bias_grad + normed * gain_grad) / counted
        return (scale_ref[0:1] * inverse * (before_grad - taken)).astype(BF16)

    grad, up, down, side = (norm_grad(ref) for ref in (joint_ref, up_ref, down_ref, side_ref))
    moved = shifted(extended(grad, up, down, side, links_ref))
    reduced = jnp.zeros((ROWS, CH), F32)
    for a in range(3):
        for b in range(3):
            reduced += dot(window(moved, a, b), dense_ref[8 - 3 * a - b], ((1,), (1,)))
    in_tile = iota((ROWS, CH), 0) % WIDE < SIDE
    reduced = jnp.where(in_tile, reduced, 0.0).astype(BF16)
    input_grad = dot(reduced, w_ref[...], ((1,), (1,))).astype(BF16)
    input_grad_ref[0] = input_grad.reshape(2, SIDE, WIDE, CH)[:, :, :SIDE, :]
    reduce_grad = dot(act, reduced, ((0,), (0,))).astype(BF16)
    packed_ref[:CH] = reduce_grad
    packed_ref[CH : 3 * CH] = expand_grad_ref[...]
    tall = [grad[t * TILE_ROWS : (t + 1) * TILE_ROWS].astype(F32) for t in range(2)]
    tall = [jnp.concatenate([own, jnp.zeros((2 * WIDE, CH), F32)], axis=0) for own in tall]
    aside = [[(pltpu.roll(own, b, 0) if b else own).astype(BF16) for own in tall] for b in range(3)]
    lowered = []
    for a in range(3):
        for b in range(3):
            parts = []
            for t in range(2):
                if a:
                    parts.append(jnp.zeros((a * WIDE, CH), BF16))
                parts.append(aside[b][t][: EXT - a * WIDE])
            lowered.append(jnp.concatenate(parts, axis=0))
    padded = jnp.concatenate([padded_ref[0], padded_ref[1]], axis=0)
    same = iota((128, 128), 0) // 8 == iota((128, 128), 1) // 8
    halves = []
    for h in range(2):
        lanes = slice(h * 128, (h + 1) * 128)
        right = jnp.concatenate([x[:, lanes] for x in lowered], axis=1)
        product = dot(padded[:, lanes], right, ((0,), (0,)))
        taps = []
        for k in range(9):
            own = jnp.where(same, product[:, k * 128 : (k + 1) * 128], 0.0)
            taps.append(jnp.sum(own.reshape(128 // 8, 8, 128), axis=0))
        halves.append(jnp.concatenate(taps, axis=0))
    taps = [jnp.concatenate(halves, axis=1)]
    group = jnp.concatenate(taps + [jnp.zeros((CH - 72, CH), F32)], axis=0).astype(BF16)
    packed_ref[3 * CH :] = group


def near_total_kernel(parts_ref, total_ref):
    total = jnp.sum(parts_ref[...].astype(F32), axis=0)
    total_ref[...] = total.reshape(total_ref.shape)


def total_kernel(parts_ref, total_ref):
    total = jnp.sum(parts_ref[...], axis=0).astype(BF16)
    total_ref[...] = jnp.broadcast_to(total[None], total_ref.shape)


def repeat_kernel(part_ref, parts_ref):
    part = part_ref[...].reshape(parts_ref.shape[1:])
    parts_ref[...] = jnp.broadcast_to(part[None], parts_ref.shape)


def unpack_kernel(packed_ref, reduce_ref, group_ref, expand_ref):
    packed = packed_ref[...].astype(F32)
    reduce_ref[...] = packed[:CH]
    expand_ref[:, :CH] = packed[CH : 2 * CH]
    expand_ref[:, CH:] = packed[2 * CH : 3 * CH]
    group_ref[...] = packed[3 * CH : 3 * CH + 72]


def body(
    sizes, activations, tissue, neighbours, w_reduce, w_group, norm_gain, norm_bias, w_expand,
    cotangent,
):
    space, near, far, first, second = sizes
    odd = (lax.axis_index(SPACE) % 2).astype(jnp.int32).reshape(1)
    rim = shape((2 * WIDE, CH), BF16)
    flat = shape((ROWS, CH), BF16)
    full = shape((ROWS, CH), F32)

    def rows_passed(top, bottom):
        up = lax.ppermute(bottom, SPACE, [(i, i + 2) for i in range(space - 2)])
        down = lax.ppermute(top, SPACE, [(i + 2, i) for i in range(space - 2)])
        return up, down

    def column_passed(column):
        return lax.ppermute(column, SPACE, [(i, i ^ 1) for i in range(space)])

    pixels = activations[0]
    beside = column_passed(jnp.stack([pixels[1, :, SIDE - 1], pixels[0, :, 0]]))
    values, top, bottom, side = call(
        reduce_kernel,
        (flat, rim, rim, shape((WIDE, CH), BF16)),
        [SMEM] + [VMEM] * 3,
        [pltpu.VMEM((2, SIDE, WIDE, CH), BF16)],
    )(odd, activations, beside, w_reduce)
    scale, mask, dense, out_grad, hidden_grad = call(
        prepare_kernel,
        (
            shape((2, CH), F32),
            shape((ROWS, 128), F32),
            shape((9, CH, CH), BF16),
            shape((ROWS, OUT), BF16),
            full,
        ),
        [VMEM] * 6,
        [pltpu.VMEM((2, SIDE, WIDE, OUT), BF16)],
    )(
        tissue, w_group, cotangent, w_expand, norm_gain.reshape(1, CH), norm_bias.reshape(1, CH)
    )
    up, down = rows_passed(top, bottom)

    width = 2 * CH + 128
    rim = shape((2 * WIDE, width), F32)
    joint, padded, sums = call(
        conv_kernel,
        (
            shape((ROWS, width), F32),
            shape((2, EXT, CH), BF16),
            shape((near, 1, width), F32),
        ),
        [SMEM] + [VMEM] * 7,
    )(neighbours, values, up, down, side, dense, mask, hidden_grad)
    parts = lax.all_to_all(sums, NEAR, 0, 0)
    sums, top, bottom = call(
        between_rows_kernel, (shape((far, 1, width), F32), rim, rim), [VMEM] * 2
    )(parts, joint)
    up, down = rows_passed(top, bottom)
    parts = lax.all_to_all(sums, FAR, 0, 0)

    expand_grad, sums = call(
        head_kernel,
        (shape((2 * CH, CH), BF16), shape((near, 1, 2 * CH), F32)),
        [VMEM] * 4,
    )(parts, joint, scale, out_grad)
    totals = lax.all_to_all(sums, NEAR, 0, 0)
    sums, column = call(
        between_column_kernel,
        (shape((far, 1, 2 * CH), F32), shape((WIDE, width), F32)),
        [SMEM] + [VMEM] * 4,
    )(odd, totals, joint, up, down)
    side = column_passed(column)
    totals = lax.all_to_all(sums, FAR, 0, 0)

    input_grad, packed, gain_grad, bias_grad = call(
        back_kernel,
        (
            shape((1, 2, SIDE, SIDE, CH), BF16),
            shape((4 * CH, CH), BF16),
            shape((1, CH), F32),
            shape((1, CH), F32),
        ),
        [SMEM] + [VMEM] * 12,
        [pltpu.VMEM((2, SIDE, WIDE, CH), BF16), pltpu.VMEM((9, CH, CH), BF16)],
    )(
        neighbours, parts, totals, joint, scale, up, down, side, w_group, padded,
        activations, w_reduce, expand_grad,
    )
    rows = packed.shape[0] // first
    share = rows // second
    parts = lax.all_to_all(packed.reshape(first, rows, CH), FIRST, 0, 0)
    total = call(near_total_kernel, shape((second, share, CH), F32), [VMEM])(parts)
    parts = lax.all_to_all(total, SECOND, 0, 0)
    total = call(total_kernel, shape((second, share, CH), BF16), [VMEM])(parts)
    part = lax.all_to_all(total, SECOND, 0, 0)
    parts = call(repeat_kernel, shape((first, rows, CH), BF16), [VMEM])(part)
    gathered = lax.all_to_all(parts, FIRST, 0, 0)
    reduce_grad, group_grad, expand_grad = call(
        unpack_kernel,
        (shape((CH, CH), F32), shape((72, CH), F32), shape((CH, OUT), F32)),
        [VMEM],
    )(gathered.reshape(packed.shape))
    return (
        input_grad,
        reduce_grad,
        group_grad.reshape(3, 3, 8, CH),
        gain_grad.reshape(CH),
        bias_grad.reshape(CH),
        expand_grad,
    )


def solution(mesh):
    dp, space = mesh.shape["dp"], mesh.shape["space"]
    zh = max(dp // 4, 1)
    zl = max(space // 16, 1)
    dims = (zh, dp // zh, zl, space // zl // 2, 2)
    cut = Mesh(mesh.devices.reshape(dims), DP + SPACE)

    def count(axes):
        return math.prod(cut.shape[axis] for axis in axes)

    sizes = tuple(count(axes) for axes in (SPACE, NEAR, FAR, FIRST, SECOND))
    return jax.shard_map(
        functools.partial(body, sizes),
        mesh=cut,
        in_specs=(
            P(DP, SPACE, None, None, None),
            P(DP, SPACE, None, None),
            P(DP, SPACE, None),
            P(),
            P(),
            P(),
            P(),
            P(),
            P(DP, SPACE, None, None, None),
        ),
        out_specs=(P(DP, SPACE, None, None, None), P(), P(), P(), P(), P()),
        check_vma=False,
    )
```

```python
import functools
import math

import jax
import jax.numpy as jnp
from jax import lax
from jax.experimental import pallas as pl
from jax.experimental.pallas import tpu as pltpu
from jax.sharding import Mesh
from jax.sharding import PartitionSpec as P

DP = ("zh", "x")
SPACE = ("zl", "y", "core")
NEAR = ("y", "core")
FAR = ("zh", "x", "zl")
FIRST = ("x", "core")
SECOND = ("zh", "zl", "y")
EPS = 1e-05
SIDE = 14
WIDE = 16
TILE_ROWS = SIDE * WIDE
ROWS = 2 * TILE_ROWS
PIXELS = 2 * SIDE * SIDE
SPARE = WIDE - 1
EXT = WIDE * WIDE
CH = 256
OUT = 512
F32 = jnp.float32
BF16 = jnp.bfloat16

VMEM = pl.BlockSpec(memory_space=pltpu.VMEM)
SMEM = pl.BlockSpec(memory_space=pltpu.SMEM)
HBM = pl.BlockSpec(memory_space=pl.ANY)
PARAMS = pltpu.CompilerParams(vmem_limit_bytes=24 * 1024 * 1024)


def call(kernel, outs, specs, scratch=()):
    return pl.pallas_call(
        kernel,
        out_shape=outs,
        in_specs=specs,
        out_specs=jax.tree.map(lambda _: VMEM, outs),
        scratch_shapes=scratch,
        compiler_params=PARAMS,
    )


def shape(dims, kind):
    return jax.ShapeDtypeStruct(dims, kind)


def dot(a, b, dims=((1,), (0,))):
    return lax.dot_general(a, b, (dims, ((), ())), preferred_element_type=F32)


def iota(dims, axis):
    return lax.broadcasted_iota(jnp.int32, dims, axis)


def rims_of(values, top_ref, bottom_ref):
    for t in range(2):
        first = t * TILE_ROWS
        last = first + TILE_ROWS - WIDE
        top_ref[t * WIDE : (t + 1) * WIDE] = values[first : first + WIDE]
        bottom_ref[t * WIDE : (t + 1) * WIDE] = values[last : last + WIDE]


def strips(values, up, down):
    out = []
    for t in range(2):
        out.append(
            jnp.concatenate(
                [
                    up[t * WIDE : (t + 1) * WIDE],
                    values[t * TILE_ROWS : (t + 1) * TILE_ROWS],
                    down[t * WIDE : (t + 1) * WIDE],
                ],
                axis=0,
            )
        )
    return out


def extended(values, up, down, side, links_ref):
    left, right = strips(values.astype(F32), up.astype(F32), down.astype(F32))
    r = iota((EXT, CH), 0) // WIDE
    c = iota((EXT, CH), 0) % WIDE
    spread_row = iota((EXT, WIDE), 0) // WIDE
    spread = (spread_row == iota((EXT, WIDE), 1)).astype(F32).astype(BF16)
    side_rows = dot(spread, side)

    def gate(t, first, middle, last):
        def on(k):
            return (links_ref[0, t, k] >= 0).astype(jnp.int32)

        level = jnp.where(r == 0, on(first), jnp.where(r == WIDE - 1, on(last), on(middle)))
        return level > 0

    out = []
    for t, own, other in ((0, left, right), (1, right, left)):
        keep = jnp.where(r == 0, (links_ref[0, t, 0] >= 0).astype(jnp.int32), 1)
        keep = jnp.where(r == WIDE - 1, (links_ref[0, t, 1] >= 0).astype(jnp.int32), keep)
        centre = pltpu.roll(jnp.where(keep > 0, own, 0.0), 1, 0)
        at_left = side_rows if t == 0 else pltpu.roll(other, EXT - (SIDE - 1), 0)
        at_right = pltpu.roll(other, WIDE - 1, 0) if t == 0 else side_rows
        value = jnp.where(c == 0, jnp.where(gate(t, 4, 2, 6), at_left, 0.0), centre)
        value = jnp.where(c == WIDE - 1, jnp.where(gate(t, 5, 3, 7), at_right, 0.0), value)
        out.append(value)
    return out


def shifted(tiles):
    moved = []
    for b in range(3):
        moved.append([(t if b == 0 else pltpu.roll(t, EXT - b, 0)).astype(BF16) for t in tiles])
    return moved


def window(moved, a, b):
    return jnp.concatenate([t[a * WIDE : a * WIDE + TILE_ROWS] for t in moved[b]], axis=0)


def reduce_kernel(
    odd_ref, act_ref, beside_ref, w_ref, values_ref, top_ref, bottom_ref, side_ref, wide
):
    wide[...] = jnp.zeros_like(wide)
    wide[:, :, :SIDE, :] = act_ref[0]
    values = dot(wide[...].reshape(ROWS, CH), w_ref[...]).astype(BF16)
    values_ref[...] = values
    down_one = iota((WIDE, SIDE), 0) == iota((WIDE, SIDE), 1) + 1
    down_one = down_one.astype(F32).astype(BF16)
    pixels = jnp.where(odd_ref[0] == 1, dot(down_one, beside_ref[0]), dot(down_one, beside_ref[1]))
    side = dot(pixels.astype(BF16), w_ref[...])
    side_ref[...] = side.astype(BF16)
    for rim_ref, first, corner in ((top_ref, 0, 1), (bottom_ref, TILE_ROWS - WIDE, SIDE)):
        strip = [values[t * TILE_ROWS + first :][:WIDE].astype(F32) for t in range(2)]
        strip = jnp.concatenate(strip, axis=0)
        spare = iota((2 * WIDE, CH), 0) == SPARE
        rim_ref[...] = jnp.where(spare, side[corner : corner + 1], strip).astype(BF16)


def spread_taps(group_ref, dense_ref):
    same = iota((CH, CH), 0) // 8 == iota((CH, CH), 1) // 8
    for tap in range(9):
        taps = group_ref[tap // 3, tap % 3].astype(F32)
        full = jnp.concatenate([taps] * (CH // 8), axis=0)
        dense_ref[tap] = jnp.where(same, full, 0.0).astype(BF16)


def prepare_kernel(
    tissue_ref, group_ref, cot_ref, expand_ref, gain_ref, bias_ref,
    scale_ref, mask_ref, dense_ref, out_grad_ref, hidden_grad_ref, wide,
):
    scale_ref[0:1] = gain_ref[...]
    scale_ref[1:2] = bias_ref[...]
    row = iota((TILE_ROWS, SIDE), 0) // WIDE
    pick = (row == iota((TILE_ROWS, SIDE), 1)).astype(F32).astype(BF16)
    col = iota((TILE_ROWS, SIDE), 0) % WIDE
    here = col == iota((TILE_ROWS, SIDE), 1)
    ones = jnp.ones((SIDE, 128), BF16)
    masks = []
    for t in range(2):
        rows = dot(pick, tissue_ref[0, t].astype(F32).astype(BF16))
        masks.append(dot(jnp.where(here, rows, 0.0).astype(BF16), ones))
    mask = jnp.concatenate(masks, axis=0)
    mask_ref[...] = mask
    spread_taps(group_ref, dense_ref)
    wide[...] = jnp.zeros_like(wide)
    wide[:, :, :SIDE, :] = cot_ref[0]
    keep = jnp.concatenate([mask] * (OUT // 128), axis=1) > 0
    out_grad = jnp.where(keep, wide[...].reshape(ROWS, OUT).astype(F32), 0.0).astype(BF16)
    out_grad_ref[...] = out_grad
    hidden_grad_ref[...] = dot(out_grad, expand_ref[...], ((1,), (1,)))


def both(mask):
    return jnp.concatenate([mask, mask], axis=1)


def conv_kernel(
    links_ref, values_ref, up_ref, down_ref, side_ref, dense_ref, mask_ref, hidden_grad_ref,
    joint_ref, padded_ref, sums_ref,
):
    up, down, side = up_ref[...], down_ref[...], side_ref[...].astype(F32)
    row = iota((WIDE, CH), 0)
    side = jnp.where(row == 0, up[SPARE : SPARE + 1].astype(F32), side)
    side = jnp.where(row == WIDE - 1, down[SPARE : SPARE + 1].astype(F32), side)
    tiles = extended(values_ref[...], up, down, side.astype(BF16), links_ref)
    for t in range(2):
        padded_ref[t] = tiles[t].astype(BF16)
    moved = shifted(tiles)
    pre = jnp.zeros((ROWS, CH), F32)
    for a in range(3):
        for b in range(3):
            pre += dot(window(moved, a, b), dense_ref[3 * a + b])
    mask = mask_ref[...]
    joint = jnp.concatenate([pre, hidden_grad_ref[...], mask], axis=1)
    joint_ref[...] = joint
    held = pre * both(mask)
    block = jnp.concatenate(
        [
            jnp.sum(held, axis=0, keepdims=True),
            jnp.sum(held * pre, axis=0, keepdims=True),
            jnp.sum(mask, axis=0, keepdims=True),
        ],
        axis=1,
    )
    sums_ref[...] = jnp.broadcast_to(block[None], sums_ref.shape)


def between_rows_kernel(parts_ref, joint_ref, sums_ref, top_ref, bottom_ref):
    between_kernel(parts_ref, sums_ref)
    rims_of(joint_ref, top_ref, bottom_ref)


def between_column_kernel(
    odd_ref, parts_ref, joint_ref, up_ref, down_ref, sums_ref, column_ref
):
    between_kernel(parts_ref, sums_ref)
    odd = odd_ref[0] == 1
    in_rim = jnp.where(odd, 0, WIDE + SIDE - 1)
    start = jnp.where(odd, 0, TILE_ROWS + SIDE - 1)
    column_ref[0:1] = up_ref[pl.ds(in_rim, 1)]
    column_ref[WIDE - 1 : WIDE] = down_ref[pl.ds(in_rim, 1)]
    for r in range(SIDE):
        column_ref[r + 1 : r + 2] = joint_ref[pl.ds(start + r * WIDE, 1)]


def between_kernel(parts_ref, sums_ref):
    block = jnp.sum(parts_ref[...], axis=0)
    sums_ref[...] = jnp.broadcast_to(block[None], sums_ref.shape)


def moments(parts_ref):
    block = jnp.sum(parts_ref[...], axis=0)
    counted = both(block[:, 2 * CH :])
    centre = block[:, :CH] / counted
    spread = block[:, CH : 2 * CH] / counted - centre * centre
    return centre, lax.rsqrt(spread + EPS), counted


def activated(normed, scale_ref):
    before = scale_ref[0:1] * normed + scale_ref[1:2]
    return before, jax.nn.sigmoid(before)


def through_silu(hidden_grad, before, sigma):
    return hidden_grad * sigma * (1.0 + before * (1.0 - sigma))


def head_kernel(
    parts_ref, joint_ref, scale_ref, out_grad_ref, expand_grad_ref, sums_ref,
):
    centre, inverse, _ = moments(parts_ref)
    normed = (joint_ref[:, :CH] - centre) * inverse
    before, sigma = activated(normed, scale_ref)
    hidden = (before * sigma).astype(BF16)
    expand_grad = dot(hidden, out_grad_ref[...], ((0,), (0,))).astype(BF16)
    expand_grad_ref[:CH] = expand_grad[:, :CH]
    expand_grad_ref[CH:] = expand_grad[:, CH:]
    before_grad = through_silu(joint_ref[:, CH : 2 * CH], before, sigma)
    gain_grad = jnp.sum(before_grad * normed, axis=0, keepdims=True)
    bias_grad = jnp.sum(before_grad, axis=0, keepdims=True)
    block = jnp.concatenate([gain_grad, bias_grad], axis=1)
    sums_ref[...] = jnp.broadcast_to(block[None], sums_ref.shape)


def back_kernel(
    links_ref, parts_ref, totals_ref, joint_ref, scale_ref,
    up_ref, down_ref, side_ref, group_ref, padded_ref, act_ref, w_ref, expand_grad_ref,
    input_grad_ref, packed_ref, gain_grad_ref, bias_grad_ref, wide, dense_ref,
):
    spread_taps(group_ref, dense_ref)
    wide[...] = jnp.zeros_like(wide)
    wide[:, :, :SIDE, :] = act_ref[0]
    act = wide[...].reshape(ROWS, CH)
    centre, inverse, counted = moments(parts_ref)
    totals = jnp.sum(totals_ref[...], axis=0)
    gain_grad = totals[:, :CH]
    bias_grad = totals[:, CH:]
    gain_grad_ref[...] = gain_grad
    bias_grad_ref[...] = bias_grad

    def norm_grad(ref):
        normed = (ref[:, :CH] - centre) * inverse
        before, sigma = activated(normed, scale_ref)
        before_grad = through_silu(ref[:, CH : 2 * CH], before, sigma)
        taken = both(ref[:, 2 * CH :]) * (bias_grad + normed * gain_grad) / counted
        return (scale_ref[0:1] * inverse * (before_grad - taken)).astype(BF16)

    grad, up, down, side = (norm_grad(ref) for ref in (joint_ref, up_ref, down_ref, side_ref))
    moved = shifted(extended(grad, up, down, side, links_ref))
    reduced = jnp.zeros((ROWS, CH), F32)
    for a in range(3):
        for b in range(3):
            reduced += dot(window(moved, a, b), dense_ref[8 - 3 * a - b], ((1,), (1,)))
    in_tile = iota((ROWS, CH), 0) % WIDE < SIDE
    reduced = jnp.where(in_tile, reduced, 0.0).astype(BF16)
    input_grad = dot(reduced, w_ref[...], ((1,), (1,))).astype(BF16)
    s = iota((PIXELS, 1), 0)
    pixel = s // 2
    wanted = s % 2 * TILE_ROWS + pixel // SIDE * WIDE + pixel % SIDE
    place = (iota((PIXELS, ROWS), 1) == wanted).astype(F32).astype(BF16)
    input_grad = dot(place, input_grad).astype(BF16)
    input_grad_ref[...] = input_grad.reshape(input_grad_ref.shape)
    reduce_grad = dot(act, reduced, ((0,), (0,))).astype(BF16)
    packed_ref[:CH] = reduce_grad
    packed_ref[CH : 3 * CH] = expand_grad_ref[...]
    tall = [grad[t * TILE_ROWS : (t + 1) * TILE_ROWS].astype(F32) for t in range(2)]
    tall = [jnp.concatenate([own, jnp.zeros((2 * WIDE, CH), F32)], axis=0) for own in tall]
    aside = [[(pltpu.roll(own, b, 0) if b else own).astype(BF16) for own in tall] for b in range(3)]
    lowered = []
    for a in range(3):
        for b in range(3):
            parts = []
            for t in range(2):
                if a:
                    parts.append(jnp.zeros((a * WIDE, CH), BF16))
                parts.append(aside[b][t][: EXT - a * WIDE])
            lowered.append(jnp.concatenate(parts, axis=0))
    padded = jnp.concatenate([padded_ref[0], padded_ref[1]], axis=0)
    same = iota((128, 128), 0) // 8 == iota((128, 128), 1) // 8
    halves = []
    for h in range(2):
        lanes = slice(h * 128, (h + 1) * 128)
        right = jnp.concatenate([x[:, lanes] for x in lowered], axis=1)
        product = dot(padded[:, lanes], right, ((0,), (0,)))
        taps = []
        for k in range(9):
            own = jnp.where(same, product[:, k * 128 : (k + 1) * 128], 0.0)
            taps.append(jnp.sum(own.reshape(128 // 8, 8, 128), axis=0))
        halves.append(jnp.concatenate(taps, axis=0))
    taps = [jnp.concatenate(halves, axis=1)]
    group = jnp.concatenate(taps + [jnp.zeros((CH - 72, CH), F32)], axis=0).astype(BF16)
    packed_ref[3 * CH :] = group


def near_total_kernel(parts_ref, total_ref):
    total = jnp.sum(parts_ref[...].astype(F32), axis=0)
    total_ref[...] = total.reshape(total_ref.shape)


def total_kernel(parts_ref, total_ref):
    total = jnp.sum(parts_ref[...], axis=0).astype(BF16)
    total_ref[...] = jnp.broadcast_to(total[None], total_ref.shape)


def repeat_kernel(part_ref, parts_ref):
    part = part_ref[...].reshape(parts_ref.shape[1:])
    parts_ref[...] = jnp.broadcast_to(part[None], parts_ref.shape)


def unpack_kernel(packed_ref, reduce_ref, group_ref, expand_ref):
    packed = packed_ref[...].astype(F32)
    reduce_ref[...] = packed[:CH]
    expand_ref[:, :CH] = packed[CH : 2 * CH]
    expand_ref[:, CH:] = packed[2 * CH : 3 * CH]
    group_ref[...] = packed[3 * CH : 3 * CH + 72]


def body(
    sizes, activations, tissue, neighbours, w_reduce, w_group, norm_gain, norm_bias, w_expand,
    cotangent,
):
    space, near, far, first, second = sizes
    odd = (lax.axis_index(SPACE) % 2).astype(jnp.int32).reshape(1)
    rim = shape((2 * WIDE, CH), BF16)
    flat = shape((ROWS, CH), BF16)
    full = shape((ROWS, CH), F32)

    def rows_passed(top, bottom):
        up = lax.ppermute(bottom, SPACE, [(i, i + 2) for i in range(space - 2)])
        down = lax.ppermute(top, SPACE, [(i + 2, i) for i in range(space - 2)])
        return up, down

    def column_passed(column):
        return lax.ppermute(column, SPACE, [(i, i ^ 1) for i in range(space)])

    pixels = activations[0]
    beside = column_passed(jnp.stack([pixels[1, :, SIDE - 1], pixels[0, :, 0]]))
    values, top, bottom, side = call(
        reduce_kernel,
        (flat, rim, rim, shape((WIDE, CH), BF16)),
        [SMEM] + [VMEM] * 3,
        [pltpu.VMEM((2, SIDE, WIDE, CH), BF16)],
    )(odd, activations, beside, w_reduce)
    scale, mask, dense, out_grad, hidden_grad = call(
        prepare_kernel,
        (
            shape((2, CH), F32),
            shape((ROWS, 128), F32),
            shape((9, CH, CH), BF16),
            shape((ROWS, OUT), BF16),
            full,
        ),
        [VMEM] * 6,
        [pltpu.VMEM((2, SIDE, WIDE, OUT), BF16)],
    )(
        tissue, w_group, cotangent, w_expand, norm_gain.reshape(1, CH), norm_bias.reshape(1, CH)
    )
    up, down = rows_passed(top, bottom)

    width = 2 * CH + 128
    rim = shape((2 * WIDE, width), F32)
    joint, padded, sums = call(
        conv_kernel,
        (
            shape((ROWS, width), F32),
            shape((2, EXT, CH), BF16),
            shape((near, 1, width), F32),
        ),
        [SMEM] + [VMEM] * 7,
    )(neighbours, values, up, down, side, dense, mask, hidden_grad)
    parts = lax.all_to_all(sums, NEAR, 0, 0)
    sums, top, bottom = call(
        between_rows_kernel, (shape((far, 1, width), F32), rim, rim), [VMEM] * 2
    )(parts, joint)
    up, down = rows_passed(top, bottom)
    parts = lax.all_to_all(sums, FAR, 0, 0)

    expand_grad, sums = call(
        head_kernel,
        (shape((2 * CH, CH), BF16), shape((near, 1, 2 * CH), F32)),
        [VMEM] * 4,
    )(parts, joint, scale, out_grad)
    totals = lax.all_to_all(sums, NEAR, 0, 0)
    sums, column = call(
        between_column_kernel,
        (shape((far, 1, 2 * CH), F32), shape((WIDE, width), F32)),
        [SMEM] + [VMEM] * 4,
    )(odd, totals, joint, up, down)
    side = column_passed(column)
    totals = lax.all_to_all(sums, FAR, 0, 0)

    input_grad, packed, gain_grad, bias_grad = call(
        back_kernel,
        (
            shape((SIDE, SIDE, 2, CH), BF16),
            shape((4 * CH, CH), BF16),
            shape((1, CH), F32),
            shape((1, CH), F32),
        ),
        [SMEM] + [VMEM] * 12,
        [pltpu.VMEM((2, SIDE, WIDE, CH), BF16), pltpu.VMEM((9, CH, CH), BF16)],
    )(
        neighbours, parts, totals, joint, scale, up, down, side, w_group, padded,
        activations, w_reduce, expand_grad,
    )
    rows = packed.shape[0] // first
    share = rows // second
    parts = lax.all_to_all(packed.reshape(first, rows, CH), FIRST, 0, 0)
    total = call(near_total_kernel, shape((second, share, CH), F32), [VMEM])(parts)
    parts = lax.all_to_all(total, SECOND, 0, 0)
    total = call(total_kernel, shape((second, share, CH), BF16), [VMEM])(parts)
    part = lax.all_to_all(total, SECOND, 0, 0)
    parts = call(repeat_kernel, shape((first, rows, CH), BF16), [VMEM])(part)
    gathered = lax.all_to_all(parts, FIRST, 0, 0)
    reduce_grad, group_grad, expand_grad = call(
        unpack_kernel,
        (shape((CH, CH), F32), shape((72, CH), F32), shape((CH, OUT), F32)),
        [VMEM],
    )(gathered.reshape(packed.shape))
    return (
        input_grad[None].transpose(0, 3, 1, 2, 4),
        reduce_grad,
        group_grad.reshape(3, 3, 8, CH),
        gain_grad.reshape(CH),
        bias_grad.reshape(CH),
        expand_grad,
    )


def solution(mesh):
    dp, space = mesh.shape["dp"], mesh.shape["space"]
    zh = max(dp // 4, 1)
    zl = max(space // 16, 1)
    dims = (zh, dp // zh, zl, space // zl // 2, 2)
    cut = Mesh(mesh.devices.reshape(dims), DP + SPACE)

    def count(axes):
        return math.prod(cut.shape[axis] for axis in axes)

    sizes = tuple(count(axes) for axes in (SPACE, NEAR, FAR, FIRST, SECOND))
    return jax.shard_map(
        functools.partial(body, sizes),
        mesh=cut,
        in_specs=(
            P(DP, SPACE, None, None, None),
            P(DP, SPACE, None, None),
            P(DP, SPACE, None),
            P(),
            P(),
            P(),
            P(),
            P(),
            P(DP, SPACE, None, None, None),
        ),
        out_specs=(P(DP, SPACE, None, None, None), P(), P(), P(), P(), P()),
        check_vma=False,
    )
```

```python
import functools
import math

import jax
import jax.numpy as jnp
from jax import lax
from jax.experimental import pallas as pl
from jax.experimental.pallas import tpu as pltpu
from jax.sharding import Mesh
from jax.sharding import PartitionSpec as P

DP = ("zh", "x")
SPACE = ("zl", "y", "core")
NEAR = ("y", "core")
FAR = ("zh", "x", "zl")
FIRST = ("x", "core")
SECOND = ("zh", "zl", "y")
EPS = 1e-05
SIDE = 14
WIDE = 16
TILE_ROWS = SIDE * WIDE
ROWS = 2 * TILE_ROWS
PIXELS = 2 * SIDE * SIDE
SPARE = WIDE - 1
EXT = WIDE * WIDE
CH = 256
OUT = 512
F32 = jnp.float32
BF16 = jnp.bfloat16

VMEM = pl.BlockSpec(memory_space=pltpu.VMEM)
SMEM = pl.BlockSpec(memory_space=pltpu.SMEM)
HBM = pl.BlockSpec(memory_space=pl.ANY)
PARAMS = pltpu.CompilerParams(vmem_limit_bytes=24 * 1024 * 1024)


def call(kernel, outs, specs, scratch=()):
    return pl.pallas_call(
        kernel,
        out_shape=outs,
        in_specs=specs,
        out_specs=jax.tree.map(lambda _: VMEM, outs),
        scratch_shapes=scratch,
        compiler_params=PARAMS,
    )


def shape(dims, kind):
    return jax.ShapeDtypeStruct(dims, kind)


def dot(a, b, dims=((1,), (0,))):
    return lax.dot_general(a, b, (dims, ((), ())), preferred_element_type=F32)


def iota(dims, axis):
    return lax.broadcasted_iota(jnp.int32, dims, axis)


def rims_of(values, top_ref, bottom_ref):
    for t in range(2):
        first = t * TILE_ROWS
        last = first + TILE_ROWS - WIDE
        top_ref[t * WIDE : (t + 1) * WIDE] = values[first : first + WIDE]
        bottom_ref[t * WIDE : (t + 1) * WIDE] = values[last : last + WIDE]


def strips(values, up, down):
    out = []
    for t in range(2):
        out.append(
            jnp.concatenate(
                [
                    up[t * WIDE : (t + 1) * WIDE],
                    values[t * TILE_ROWS : (t + 1) * TILE_ROWS],
                    down[t * WIDE : (t + 1) * WIDE],
                ],
                axis=0,
            )
        )
    return out


def extended(values, up, down, side, links_ref):
    left, right = strips(values.astype(F32), up.astype(F32), down.astype(F32))
    r = iota((EXT, CH), 0) // WIDE
    c = iota((EXT, CH), 0) % WIDE
    spread_row = iota((EXT, WIDE), 0) // WIDE
    spread = (spread_row == iota((EXT, WIDE), 1)).astype(F32).astype(BF16)
    side_rows = dot(spread, side)

    def gate(t, first, middle, last):
        def on(k):
            return (links_ref[0, t, k] >= 0).astype(jnp.int32)

        level = jnp.where(r == 0, on(first), jnp.where(r == WIDE - 1, on(last), on(middle)))
        return level > 0

    out = []
    for t, own, other in ((0, left, right), (1, right, left)):
        keep = jnp.where(r == 0, (links_ref[0, t, 0] >= 0).astype(jnp.int32), 1)
        keep = jnp.where(r == WIDE - 1, (links_ref[0, t, 1] >= 0).astype(jnp.int32), keep)
        centre = pltpu.roll(jnp.where(keep > 0, own, 0.0), 1, 0)
        at_left = side_rows if t == 0 else pltpu.roll(other, EXT - (SIDE - 1), 0)
        at_right = pltpu.roll(other, WIDE - 1, 0) if t == 0 else side_rows
        value = jnp.where(c == 0, jnp.where(gate(t, 4, 2, 6), at_left, 0.0), centre)
        value = jnp.where(c == WIDE - 1, jnp.where(gate(t, 5, 3, 7), at_right, 0.0), value)
        out.append(value)
    return out


def shifted(tiles):
    moved = []
    for b in range(3):
        moved.append([(t if b == 0 else pltpu.roll(t, EXT - b, 0)).astype(BF16) for t in tiles])
    return moved


def window(moved, a, b):
    return jnp.concatenate([t[a * WIDE : a * WIDE + TILE_ROWS] for t in moved[b]], axis=0)


def reduce_kernel(
    odd_ref, act_ref, beside_ref, w_ref, values_ref, top_ref, bottom_ref, side_ref, wide
):
    wide[...] = jnp.zeros_like(wide)
    wide[:, :, :SIDE, :] = act_ref[0]
    values = dot(wide[...].reshape(ROWS, CH), w_ref[...]).astype(BF16)
    values_ref[...] = values
    down_one = iota((WIDE, SIDE), 0) == iota((WIDE, SIDE), 1) + 1
    down_one = down_one.astype(F32).astype(BF16)
    pixels = jnp.where(odd_ref[0] == 1, dot(down_one, beside_ref[0]), dot(down_one, beside_ref[1]))
    side = dot(pixels.astype(BF16), w_ref[...])
    side_ref[...] = side.astype(BF16)
    for rim_ref, first, corner in ((top_ref, 0, 1), (bottom_ref, TILE_ROWS - WIDE, SIDE)):
        strip = [values[t * TILE_ROWS + first :][:WIDE].astype(F32) for t in range(2)]
        strip = jnp.concatenate(strip, axis=0)
        spare = iota((2 * WIDE, CH), 0) == SPARE
        rim_ref[...] = jnp.where(spare, side[corner : corner + 1], strip).astype(BF16)


def spread_taps(group_ref, dense_ref):
    same = iota((CH, CH), 0) // 8 == iota((CH, CH), 1) // 8
    for tap in range(9):
        taps = group_ref[tap // 3, tap % 3].astype(F32)
        full = jnp.concatenate([taps] * (CH // 8), axis=0)
        dense_ref[tap] = jnp.where(same, full, 0.0).astype(BF16)


def prepare_kernel(
    tissue_ref, group_ref, cot_ref, expand_ref, gain_ref, bias_ref,
    scale_ref, mask_ref, dense_ref, out_grad_ref, hidden_grad_ref, wide,
):
    scale_ref[0:1] = gain_ref[...]
    scale_ref[1:2] = bias_ref[...]
    row = iota((TILE_ROWS, SIDE), 0) // WIDE
    pick = (row == iota((TILE_ROWS, SIDE), 1)).astype(F32).astype(BF16)
    col = iota((TILE_ROWS, SIDE), 0) % WIDE
    here = col == iota((TILE_ROWS, SIDE), 1)
    ones = jnp.ones((SIDE, 128), BF16)
    masks = []
    for t in range(2):
        rows = dot(pick, tissue_ref[0, t].astype(F32).astype(BF16))
        masks.append(dot(jnp.where(here, rows, 0.0).astype(BF16), ones))
    mask = jnp.concatenate(masks, axis=0)
    mask_ref[...] = mask
    spread_taps(group_ref, dense_ref)
    wide[...] = jnp.zeros_like(wide)
    wide[:, :, :SIDE, :] = cot_ref[0]
    keep = jnp.concatenate([mask] * (OUT // 128), axis=1) > 0
    out_grad = jnp.where(keep, wide[...].reshape(ROWS, OUT).astype(F32), 0.0).astype(BF16)
    out_grad_ref[...] = out_grad
    hidden_grad_ref[...] = dot(out_grad, expand_ref[...], ((1,), (1,)))


def both(mask):
    return jnp.concatenate([mask, mask], axis=1)


def conv_kernel(
    links_ref, values_ref, up_ref, down_ref, side_ref, dense_ref, mask_ref, hidden_grad_ref,
    joint_ref, padded_ref, sums_ref,
):
    up, down, side = up_ref[...], down_ref[...], side_ref[...].astype(F32)
    row = iota((WIDE, CH), 0)
    side = jnp.where(row == 0, up[SPARE : SPARE + 1].astype(F32), side)
    side = jnp.where(row == WIDE - 1, down[SPARE : SPARE + 1].astype(F32), side)
    tiles = extended(values_ref[...], up, down, side.astype(BF16), links_ref)
    for t in range(2):
        padded_ref[t] = tiles[t].astype(BF16)
    moved = shifted(tiles)
    pre = jnp.zeros((ROWS, CH), F32)
    for a in range(3):
        for b in range(3):
            pre += dot(window(moved, a, b), dense_ref[3 * a + b])
    mask = mask_ref[...]
    joint = jnp.concatenate([pre, hidden_grad_ref[...], mask], axis=1)
    joint_ref[...] = joint
    held = pre * both(mask)
    block = jnp.concatenate(
        [
            jnp.sum(held, axis=0, keepdims=True),
            jnp.sum(held * pre, axis=0, keepdims=True),
            jnp.sum(mask, axis=0, keepdims=True),
        ],
        axis=1,
    )
    sums_ref[...] = jnp.broadcast_to(block[None], sums_ref.shape)


def between_rows_kernel(parts_ref, joint_ref, sums_ref, top_ref, bottom_ref):
    between_kernel(parts_ref, sums_ref)
    rims_of(joint_ref, top_ref, bottom_ref)


def between_column_kernel(
    odd_ref, parts_ref, joint_ref, up_ref, down_ref, sums_ref, column_ref
):
    between_kernel(parts_ref, sums_ref)
    odd = odd_ref[0] == 1
    in_rim = jnp.where(odd, 0, WIDE + SIDE - 1)
    start = jnp.where(odd, 0, TILE_ROWS + SIDE - 1)
    column_ref[0:1] = up_ref[pl.ds(in_rim, 1)]
    column_ref[WIDE - 1 : WIDE] = down_ref[pl.ds(in_rim, 1)]
    for r in range(SIDE):
        column_ref[r + 1 : r + 2] = joint_ref[pl.ds(start + r * WIDE, 1)]


def between_kernel(parts_ref, sums_ref):
    block = jnp.sum(parts_ref[...], axis=0)
    sums_ref[...] = jnp.broadcast_to(block[None], sums_ref.shape)


def moments(parts_ref):
    block = jnp.sum(parts_ref[...], axis=0)
    counted = both(block[:, 2 * CH :])
    centre = block[:, :CH] / counted
    spread = block[:, CH : 2 * CH] / counted - centre * centre
    return centre, lax.rsqrt(spread + EPS), counted


def activated(normed, scale_ref):
    before = scale_ref[0:1] * normed + scale_ref[1:2]
    return before, jax.nn.sigmoid(before)


def through_silu(hidden_grad, before, sigma):
    return hidden_grad * sigma * (1.0 + before * (1.0 - sigma))


def head_kernel(
    parts_ref, joint_ref, scale_ref, out_grad_ref, expand_grad_ref, sums_ref,
):
    centre, inverse, _ = moments(parts_ref)
    normed = (joint_ref[:, :CH] - centre) * inverse
    before, sigma = activated(normed, scale_ref)
    hidden = (before * sigma).astype(BF16)
    expand_grad = dot(hidden, out_grad_ref[...], ((0,), (0,))).astype(BF16)
    expand_grad_ref[:CH] = expand_grad[:, :CH]
    expand_grad_ref[CH:] = expand_grad[:, CH:]
    before_grad = through_silu(joint_ref[:, CH : 2 * CH], before, sigma)
    gain_grad = jnp.sum(before_grad * normed, axis=0, keepdims=True)
    bias_grad = jnp.sum(before_grad, axis=0, keepdims=True)
    block = jnp.concatenate([gain_grad, bias_grad], axis=1)
    sums_ref[...] = jnp.broadcast_to(block[None], sums_ref.shape)


def back_kernel(
    links_ref, parts_ref, totals_ref, joint_ref, scale_ref,
    up_ref, down_ref, side_ref, group_ref, padded_ref, act_ref, w_ref, expand_grad_ref,
    input_grad_ref, packed_ref, gain_grad_ref, bias_grad_ref, wide, dense_ref,
):
    spread_taps(group_ref, dense_ref)
    wide[...] = jnp.zeros_like(wide)
    wide[:, :, :SIDE, :] = act_ref[0]
    act = wide[...].reshape(ROWS, CH)
    centre, inverse, counted = moments(parts_ref)
    totals = jnp.sum(totals_ref[...], axis=0)
    gain_grad = totals[:, :CH]
    bias_grad = totals[:, CH:]
    gain_grad_ref[...] = gain_grad
    bias_grad_ref[...] = bias_grad

    def norm_grad(ref):
        normed = (ref[:, :CH] - centre) * inverse
        before, sigma = activated(normed, scale_ref)
        before_grad = through_silu(ref[:, CH : 2 * CH], before, sigma)
        taken = both(ref[:, 2 * CH :]) * (bias_grad + normed * gain_grad) / counted
        return (scale_ref[0:1] * inverse * (before_grad - taken)).astype(BF16)

    grad, up, down, side = (norm_grad(ref) for ref in (joint_ref, up_ref, down_ref, side_ref))
    moved = shifted(extended(grad, up, down, side, links_ref))
    reduced = jnp.zeros((ROWS, CH), F32)
    for a in range(3):
        for b in range(3):
            reduced += dot(window(moved, a, b), dense_ref[8 - 3 * a - b], ((1,), (1,)))
    in_tile = iota((ROWS, CH), 0) % WIDE < SIDE
    reduced = jnp.where(in_tile, reduced, 0.0).astype(BF16)
    input_grad = dot(reduced, w_ref[...], ((1,), (1,))).astype(BF16)
    s = iota((PIXELS, 1), 0)
    pixel = s // 2
    wanted = s % 2 * TILE_ROWS + pixel // SIDE * WIDE + pixel % SIDE
    place = (iota((PIXELS, ROWS), 1) == wanted).astype(F32).astype(BF16)
    input_grad = dot(place, input_grad).astype(BF16)
    input_grad_ref[...] = input_grad.reshape(input_grad_ref.shape)
    reduce_grad = dot(act, reduced, ((0,), (0,))).astype(BF16)
    packed_ref[:CH] = reduce_grad
    packed_ref[CH : 3 * CH] = expand_grad_ref[...]
    tall = [grad[t * TILE_ROWS : (t + 1) * TILE_ROWS].astype(F32) for t in range(2)]
    tall = [jnp.concatenate([own, jnp.zeros((2 * WIDE, CH), F32)], axis=0) for own in tall]
    aside = [[(pltpu.roll(own, b, 0) if b else own).astype(BF16) for own in tall] for b in range(3)]
    lowered = []
    for a in range(3):
        for b in range(3):
            parts = []
            for t in range(2):
                if a:
                    parts.append(jnp.zeros((a * WIDE, CH), BF16))
                parts.append(aside[b][t][: EXT - a * WIDE])
            lowered.append(jnp.concatenate(parts, axis=0))
    padded = jnp.concatenate([padded_ref[0], padded_ref[1]], axis=0)
    same = iota((128, 128), 0) // 8 == iota((128, 128), 1) // 8
    halves = []
    for h in range(2):
        lanes = slice(h * 128, (h + 1) * 128)
        right = jnp.concatenate([x[:, lanes] for x in lowered], axis=1)
        product = dot(padded[:, lanes], right, ((0,), (0,)))
        taps = []
        for k in range(9):
            own = jnp.where(same, product[:, k * 128 : (k + 1) * 128], 0.0)
            taps.append(jnp.sum(own.reshape(128 // 8, 8, 128), axis=0))
        halves.append(jnp.concatenate(taps, axis=0))
    taps = [jnp.concatenate(halves, axis=1)]
    group = jnp.concatenate(taps + [jnp.zeros((CH - 72, CH), F32)], axis=0).astype(BF16)
    packed_ref[3 * CH :] = group[: packed_ref.shape[0] - 3 * CH]


def near_total_kernel(parts_ref, total_ref):
    total = jnp.sum(parts_ref[...].astype(F32), axis=0)
    spare = total_ref.shape[0] * total_ref.shape[1] - total.shape[0]
    if spare:
        total = jnp.concatenate([total, jnp.zeros((spare, CH), F32)], axis=0)
    total_ref[...] = total.reshape(total_ref.shape)


def total_kernel(parts_ref, total_ref):
    total = jnp.sum(parts_ref[...], axis=0).astype(BF16)
    total_ref[...] = jnp.broadcast_to(total[None], total_ref.shape)


def repeat_kernel(part_ref, parts_ref):
    part = part_ref[...].reshape(part_ref.shape[0] * part_ref.shape[1], CH)
    part = part[: parts_ref.shape[1]]
    parts_ref[...] = jnp.broadcast_to(part[None], parts_ref.shape)


def unpack_kernel(packed_ref, reduce_ref, group_ref, expand_ref):
    packed = packed_ref[...].astype(F32)
    reduce_ref[...] = packed[:CH]
    expand_ref[:, :CH] = packed[CH : 2 * CH]
    expand_ref[:, CH:] = packed[2 * CH : 3 * CH]
    group_ref[...] = packed[3 * CH : 3 * CH + 72]


def body(
    sizes, activations, tissue, neighbours, w_reduce, w_group, norm_gain, norm_bias, w_expand,
    cotangent,
):
    space, near, far, first, second = sizes
    odd = (lax.axis_index(SPACE) % 2).astype(jnp.int32).reshape(1)
    rim = shape((2 * WIDE, CH), BF16)
    flat = shape((ROWS, CH), BF16)
    full = shape((ROWS, CH), F32)

    def rows_passed(top, bottom):
        up = lax.ppermute(bottom, SPACE, [(i, i + 2) for i in range(space - 2)])
        down = lax.ppermute(top, SPACE, [(i + 2, i) for i in range(space - 2)])
        return up, down

    def column_passed(column):
        return lax.ppermute(column, SPACE, [(i, i ^ 1) for i in range(space)])

    pixels = activations[0]
    beside = column_passed(jnp.stack([pixels[1, :, SIDE - 1], pixels[0, :, 0]]))
    values, top, bottom, side = call(
        reduce_kernel,
        (flat, rim, rim, shape((WIDE, CH), BF16)),
        [SMEM] + [VMEM] * 3,
        [pltpu.VMEM((2, SIDE, WIDE, CH), BF16)],
    )(odd, activations, beside, w_reduce)
    scale, mask, dense, out_grad, hidden_grad = call(
        prepare_kernel,
        (
            shape((2, CH), F32),
            shape((ROWS, 128), F32),
            shape((9, CH, CH), BF16),
            shape((ROWS, OUT), BF16),
            full,
        ),
        [VMEM] * 6,
        [pltpu.VMEM((2, SIDE, WIDE, OUT), BF16)],
    )(
        tissue, w_group, cotangent, w_expand, norm_gain.reshape(1, CH), norm_bias.reshape(1, CH)
    )
    up, down = rows_passed(top, bottom)

    width = 2 * CH + 128
    rim = shape((2 * WIDE, width), F32)
    joint, padded, sums = call(
        conv_kernel,
        (
            shape((ROWS, width), F32),
            shape((2, EXT, CH), BF16),
            shape((near, 1, width), F32),
        ),
        [SMEM] + [VMEM] * 7,
    )(neighbours, values, up, down, side, dense, mask, hidden_grad)
    parts = lax.all_to_all(sums, NEAR, 0, 0)
    sums, top, bottom = call(
        between_rows_kernel, (shape((far, 1, width), F32), rim, rim), [VMEM] * 2
    )(parts, joint)
    up, down = rows_passed(top, bottom)
    parts = lax.all_to_all(sums, FAR, 0, 0)

    expand_grad, sums = call(
        head_kernel,
        (shape((2 * CH, CH), BF16), shape((near, 1, 2 * CH), F32)),
        [VMEM] * 4,
    )(parts, joint, scale, out_grad)
    totals = lax.all_to_all(sums, NEAR, 0, 0)
    sums, column = call(
        between_column_kernel,
        (shape((far, 1, 2 * CH), F32), shape((WIDE, width), F32)),
        [SMEM] + [VMEM] * 4,
    )(odd, totals, joint, up, down)
    side = column_passed(column)
    totals = lax.all_to_all(sums, FAR, 0, 0)

    rows = pl.cdiv(3 * CH + 72, first * 16) * 16
    share = pl.cdiv(rows, second)
    input_grad, packed, gain_grad, bias_grad = call(
        back_kernel,
        (
            shape((SIDE, SIDE, 2, CH), BF16),
            shape((first * rows, CH), BF16),
            shape((1, CH), F32),
            shape((1, CH), F32),
        ),
        [SMEM] + [VMEM] * 12,
        [pltpu.VMEM((2, SIDE, WIDE, CH), BF16), pltpu.VMEM((9, CH, CH), BF16)],
    )(
        neighbours, parts, totals, joint, scale, up, down, side, w_group, padded,
        activations, w_reduce, expand_grad,
    )
    parts = lax.all_to_all(packed.reshape(first, rows, CH), FIRST, 0, 0)
    total = call(near_total_kernel, shape((second, share, CH), F32), [VMEM])(parts)
    parts = lax.all_to_all(total, SECOND, 0, 0)
    total = call(total_kernel, shape((second, share, CH), BF16), [VMEM])(parts)
    part = lax.all_to_all(total, SECOND, 0, 0)
    parts = call(repeat_kernel, shape((first, rows, CH), BF16), [VMEM])(part)
    gathered = lax.all_to_all(parts, FIRST, 0, 0)
    reduce_grad, group_grad, expand_grad = call(
        unpack_kernel,
        (shape((CH, CH), F32), shape((72, CH), F32), shape((CH, OUT), F32)),
        [VMEM],
    )(gathered.reshape(packed.shape))
    return (
        input_grad[None].transpose(0, 3, 1, 2, 4),
        reduce_grad,
        group_grad.reshape(3, 3, 8, CH),
        gain_grad.reshape(CH),
        bias_grad.reshape(CH),
        expand_grad,
    )


def solution(mesh):
    dp, space = mesh.shape["dp"], mesh.shape["space"]
    zh = max(dp // 4, 1)
    zl = max(space // 16, 1)
    dims = (zh, dp // zh, zl, space // zl // 2, 2)
    cut = Mesh(mesh.devices.reshape(dims), DP + SPACE)

    def count(axes):
        return math.prod(cut.shape[axis] for axis in axes)

    sizes = tuple(count(axes) for axes in (SPACE, NEAR, FAR, FIRST, SECOND))
    return jax.shard_map(
        functools.partial(body, sizes),
        mesh=cut,
        in_specs=(
            P(DP, SPACE, None, None, None),
            P(DP, SPACE, None, None),
            P(DP, SPACE, None),
            P(),
            P(),
            P(),
            P(),
            P(),
            P(DP, SPACE, None, None, None),
        ),
        out_specs=(P(DP, SPACE, None, None, None), P(), P(), P(), P(), P()),
        check_vma=False,
    )
```

```python
import functools
import math

import jax
import jax.numpy as jnp
from jax import lax
from jax.experimental import pallas as pl
from jax.experimental.pallas import tpu as pltpu
from jax.sharding import Mesh
from jax.sharding import PartitionSpec as P

DP = ("zh", "x")
SPACE = ("zl", "y", "core")
NEAR = ("y", "core")
FAR = ("zh", "x", "zl")
FIRST = ("x", "core")
SECOND = ("zh", "zl", "y")
EPS = 1e-05
SIDE = 14
WIDE = 16
TILE_ROWS = SIDE * WIDE
ROWS = 2 * TILE_ROWS
PIXELS = 2 * SIDE * SIDE
SPARE = WIDE - 1
EXT = WIDE * WIDE
CH = 256
OUT = 512
F32 = jnp.float32
BF16 = jnp.bfloat16

VMEM = pl.BlockSpec(memory_space=pltpu.VMEM)
SMEM = pl.BlockSpec(memory_space=pltpu.SMEM)
HBM = pl.BlockSpec(memory_space=pl.ANY)
PARAMS = pltpu.CompilerParams(vmem_limit_bytes=24 * 1024 * 1024)


def call(kernel, outs, specs, scratch=()):
    return pl.pallas_call(
        kernel,
        out_shape=outs,
        in_specs=specs,
        out_specs=jax.tree.map(lambda _: VMEM, outs),
        scratch_shapes=scratch,
        compiler_params=PARAMS,
    )


def shape(dims, kind):
    return jax.ShapeDtypeStruct(dims, kind)


def dot(a, b, dims=((1,), (0,))):
    return lax.dot_general(a, b, (dims, ((), ())), preferred_element_type=F32)


def iota(dims, axis):
    return lax.broadcasted_iota(jnp.int32, dims, axis)


def rims_of(values, top_ref, bottom_ref):
    for t in range(2):
        first = t * TILE_ROWS
        last = first + TILE_ROWS - WIDE
        top_ref[t * WIDE : (t + 1) * WIDE] = values[first : first + WIDE]
        bottom_ref[t * WIDE : (t + 1) * WIDE] = values[last : last + WIDE]


def strips(values, up, down):
    out = []
    for t in range(2):
        out.append(
            jnp.concatenate(
                [
                    up[t * WIDE : (t + 1) * WIDE],
                    values[t * TILE_ROWS : (t + 1) * TILE_ROWS],
                    down[t * WIDE : (t + 1) * WIDE],
                ],
                axis=0,
            )
        )
    return out


def extended(values, up, down, side, links_ref):
    left, right = strips(values.astype(F32), up.astype(F32), down.astype(F32))
    r = iota((EXT, CH), 0) // WIDE
    c = iota((EXT, CH), 0) % WIDE
    spread_row = iota((EXT, WIDE), 0) // WIDE
    spread = (spread_row == iota((EXT, WIDE), 1)).astype(F32).astype(BF16)
    side_rows = dot(spread, side)

    def gate(t, first, middle, last):
        def on(k):
            return (links_ref[0, t, k] >= 0).astype(jnp.int32)

        level = jnp.where(r == 0, on(first), jnp.where(r == WIDE - 1, on(last), on(middle)))
        return level > 0

    out = []
    for t, own, other in ((0, left, right), (1, right, left)):
        keep = jnp.where(r == 0, (links_ref[0, t, 0] >= 0).astype(jnp.int32), 1)
        keep = jnp.where(r == WIDE - 1, (links_ref[0, t, 1] >= 0).astype(jnp.int32), keep)
        centre = pltpu.roll(jnp.where(keep > 0, own, 0.0), 1, 0)
        at_left = side_rows if t == 0 else pltpu.roll(other, EXT - (SIDE - 1), 0)
        at_right = pltpu.roll(other, WIDE - 1, 0) if t == 0 else side_rows
        value = jnp.where(c == 0, jnp.where(gate(t, 4, 2, 6), at_left, 0.0), centre)
        value = jnp.where(c == WIDE - 1, jnp.where(gate(t, 5, 3, 7), at_right, 0.0), value)
        out.append(value)
    return out


def shifted(tiles):
    moved = []
    for b in range(3):
        moved.append([(t if b == 0 else pltpu.roll(t, EXT - b, 0)).astype(BF16) for t in tiles])
    return moved


def window(moved, a, b):
    return jnp.concatenate([t[a * WIDE : a * WIDE + TILE_ROWS] for t in moved[b]], axis=0)


def reduce_kernel(
    odd_ref, act_ref, beside_ref, w_ref, values_ref, top_ref, bottom_ref, side_ref, wide
):
    wide[...] = jnp.zeros_like(wide)
    wide[:, :, :SIDE, :] = act_ref[0]
    values = dot(wide[...].reshape(ROWS, CH), w_ref[...]).astype(BF16)
    values_ref[...] = values
    down_one = iota((WIDE, SIDE), 0) == iota((WIDE, SIDE), 1) + 1
    down_one = down_one.astype(F32).astype(BF16)
    pixels = jnp.where(odd_ref[0] == 1, dot(down_one, beside_ref[0]), dot(down_one, beside_ref[1]))
    side = dot(pixels.astype(BF16), w_ref[...])
    side_ref[...] = side.astype(BF16)
    for rim_ref, first, corner in ((top_ref, 0, 1), (bottom_ref, TILE_ROWS - WIDE, SIDE)):
        strip = [values[t * TILE_ROWS + first :][:WIDE].astype(F32) for t in range(2)]
        strip = jnp.concatenate(strip, axis=0)
        spare = iota((2 * WIDE, CH), 0) == SPARE
        rim_ref[...] = jnp.where(spare, side[corner : corner + 1], strip).astype(BF16)


def spread_taps(group_ref, dense_ref):
    same = iota((CH, CH), 0) // 8 == iota((CH, CH), 1) // 8
    for tap in range(9):
        taps = group_ref[tap // 3, tap % 3].astype(F32)
        full = jnp.concatenate([taps] * (CH // 8), axis=0)
        dense_ref[tap] = jnp.where(same, full, 0.0).astype(BF16)


def prepare_kernel(
    tissue_ref, group_ref, cot_ref, expand_ref, gain_ref, bias_ref,
    scale_ref, mask_ref, dense_ref, out_grad_ref, hidden_grad_ref, wide,
):
    scale_ref[0:1] = gain_ref[...]
    scale_ref[1:2] = bias_ref[...]
    row = iota((TILE_ROWS, SIDE), 0) // WIDE
    pick = (row == iota((TILE_ROWS, SIDE), 1)).astype(F32).astype(BF16)
    col = iota((TILE_ROWS, SIDE), 0) % WIDE
    here = col == iota((TILE_ROWS, SIDE), 1)
    ones = jnp.ones((SIDE, 128), BF16)
    masks = []
    for t in range(2):
        rows = dot(pick, tissue_ref[0, t].astype(F32).astype(BF16))
        masks.append(dot(jnp.where(here, rows, 0.0).astype(BF16), ones))
    mask = jnp.concatenate(masks, axis=0)
    mask_ref[...] = mask
    spread_taps(group_ref, dense_ref)
    wide[...] = jnp.zeros_like(wide)
    wide[:, :, :SIDE, :] = cot_ref[0]
    keep = jnp.concatenate([mask] * (OUT // 128), axis=1) > 0
    out_grad = jnp.where(keep, wide[...].reshape(ROWS, OUT).astype(F32), 0.0).astype(BF16)
    out_grad_ref[...] = out_grad
    hidden_grad_ref[...] = dot(out_grad, expand_ref[...], ((1,), (1,)))


def both(mask):
    return jnp.concatenate([mask, mask], axis=1)


def conv_kernel(
    links_ref, values_ref, up_ref, down_ref, side_ref, dense_ref, mask_ref, hidden_grad_ref,
    joint_ref, padded_ref, sums_ref,
):
    up, down, side = up_ref[...], down_ref[...], side_ref[...].astype(F32)
    row = iota((WIDE, CH), 0)
    side = jnp.where(row == 0, up[SPARE : SPARE + 1].astype(F32), side)
    side = jnp.where(row == WIDE - 1, down[SPARE : SPARE + 1].astype(F32), side)
    tiles = extended(values_ref[...], up, down, side.astype(BF16), links_ref)
    for t in range(2):
        padded_ref[t] = tiles[t].astype(BF16)
    moved = shifted(tiles)
    pre = jnp.zeros((ROWS, CH), F32)
    for a in range(3):
        for b in range(3):
            pre += dot(window(moved, a, b), dense_ref[3 * a + b])
    mask = mask_ref[...]
    joint = jnp.concatenate([pre, hidden_grad_ref[...], mask], axis=1)
    joint_ref[...] = joint
    held = pre * both(mask)
    block = jnp.concatenate(
        [
            jnp.sum(held, axis=0, keepdims=True),
            jnp.sum(held * pre, axis=0, keepdims=True),
            jnp.sum(mask, axis=0, keepdims=True),
        ],
        axis=1,
    )
    sums_ref[...] = jnp.broadcast_to(block[None], sums_ref.shape)


def between_rows_kernel(parts_ref, joint_ref, sums_ref, top_ref, bottom_ref):
    between_kernel(parts_ref, sums_ref)
    rims_of(joint_ref, top_ref, bottom_ref)


def between_column_kernel(
    odd_ref, parts_ref, joint_ref, up_ref, down_ref, sums_ref, column_ref
):
    between_kernel(parts_ref, sums_ref)
    odd = odd_ref[0] == 1
    in_rim = jnp.where(odd, 0, WIDE + SIDE - 1)
    start = jnp.where(odd, 0, TILE_ROWS + SIDE - 1)
    column_ref[0:1] = up_ref[pl.ds(in_rim, 1)]
    column_ref[WIDE - 1 : WIDE] = down_ref[pl.ds(in_rim, 1)]
    for r in range(SIDE):
        column_ref[r + 1 : r + 2] = joint_ref[pl.ds(start + r * WIDE, 1)]


def between_kernel(parts_ref, sums_ref):
    block = jnp.sum(parts_ref[...], axis=0)
    sums_ref[...] = jnp.broadcast_to(block[None], sums_ref.shape)


def moments(parts_ref):
    block = jnp.sum(parts_ref[...], axis=0)
    counted = both(block[:, 2 * CH :])
    centre = block[:, :CH] / counted
    spread = block[:, CH : 2 * CH] / counted - centre * centre
    return centre, lax.rsqrt(spread + EPS), counted


def activated(normed, scale_ref):
    before = scale_ref[0:1] * normed + scale_ref[1:2]
    return before, jax.nn.sigmoid(before)


def through_silu(hidden_grad, before, sigma):
    return hidden_grad * sigma * (1.0 + before * (1.0 - sigma))


def head_kernel(
    parts_ref, joint_ref, scale_ref, out_grad_ref, expand_grad_ref, sums_ref,
):
    centre, inverse, _ = moments(parts_ref)
    normed = (joint_ref[:, :CH] - centre) * inverse
    before, sigma = activated(normed, scale_ref)
    hidden = (before * sigma).astype(BF16)
    expand_grad = dot(hidden, out_grad_ref[...], ((0,), (0,))).astype(BF16)
    expand_grad_ref[:CH] = expand_grad[:, :CH]
    expand_grad_ref[CH:] = expand_grad[:, CH:]
    before_grad = through_silu(joint_ref[:, CH : 2 * CH], before, sigma)
    gain_grad = jnp.sum(before_grad * normed, axis=0, keepdims=True)
    bias_grad = jnp.sum(before_grad, axis=0, keepdims=True)
    block = jnp.concatenate([gain_grad, bias_grad], axis=1)
    sums_ref[...] = jnp.broadcast_to(block[None], sums_ref.shape)


def back_kernel(
    links_ref, parts_ref, totals_ref, joint_ref, scale_ref,
    up_ref, down_ref, side_ref, group_ref, padded_ref, act_ref, w_ref, expand_grad_ref,
    input_grad_ref, packed_ref, gain_grad_ref, bias_grad_ref, wide, dense_ref,
):
    spread_taps(group_ref, dense_ref)
    wide[...] = jnp.zeros_like(wide)
    wide[:, :, :SIDE, :] = act_ref[0]
    act = wide[...].reshape(ROWS, CH)
    centre, inverse, counted = moments(parts_ref)
    totals = jnp.sum(totals_ref[...], axis=0)
    gain_grad = totals[:, :CH]
    bias_grad = totals[:, CH:]
    gain_grad_ref[...] = gain_grad
    bias_grad_ref[...] = bias_grad

    def norm_grad(ref):
        normed = (ref[:, :CH] - centre) * inverse
        before, sigma = activated(normed, scale_ref)
        before_grad = through_silu(ref[:, CH : 2 * CH], before, sigma)
        taken = both(ref[:, 2 * CH :]) * (bias_grad + normed * gain_grad) / counted
        return (scale_ref[0:1] * inverse * (before_grad - taken)).astype(BF16)

    grad, up, down, side = (norm_grad(ref) for ref in (joint_ref, up_ref, down_ref, side_ref))
    moved = shifted(extended(grad, up, down, side, links_ref))
    reduced = jnp.zeros((ROWS, CH), F32)
    for a in range(3):
        for b in range(3):
            reduced += dot(window(moved, a, b), dense_ref[8 - 3 * a - b], ((1,), (1,)))
    in_tile = iota((ROWS, CH), 0) % WIDE < SIDE
    reduced = jnp.where(in_tile, reduced, 0.0).astype(BF16)
    input_grad = dot(reduced, w_ref[...], ((1,), (1,))).astype(BF16)
    s = iota((PIXELS, 1), 0)
    pixel = s // 2
    wanted = s % 2 * TILE_ROWS + pixel // SIDE * WIDE + pixel % SIDE
    place = (iota((PIXELS, ROWS), 1) == wanted).astype(F32).astype(BF16)
    input_grad = dot(place, input_grad).astype(BF16)
    input_grad_ref[...] = input_grad.reshape(input_grad_ref.shape)
    reduce_grad = dot(act, reduced, ((0,), (0,))).astype(BF16)
    packed_ref[:CH] = reduce_grad
    packed_ref[CH : 3 * CH] = expand_grad_ref[...]
    tall = [grad[t * TILE_ROWS : (t + 1) * TILE_ROWS].astype(F32) for t in range(2)]
    tall = [jnp.concatenate([own, jnp.zeros((2 * WIDE, CH), F32)], axis=0) for own in tall]
    aside = [[(pltpu.roll(own, b, 0) if b else own).astype(BF16) for own in tall] for b in range(3)]
    lowered = []
    for a in range(3):
        for b in range(3):
            parts = []
            for t in range(2):
                if a:
                    parts.append(jnp.zeros((a * WIDE, CH), BF16))
                parts.append(aside[b][t][: EXT - a * WIDE])
            lowered.append(jnp.concatenate(parts, axis=0))
    padded = jnp.concatenate([padded_ref[0], padded_ref[1]], axis=0)
    same = iota((128, 128), 0) // 8 == iota((128, 128), 1) // 8
    halves = []
    for h in range(2):
        lanes = slice(h * 128, (h + 1) * 128)
        right = jnp.concatenate([x[:, lanes] for x in lowered], axis=1)
        product = dot(padded[:, lanes], right, ((0,), (0,)))
        taps = []
        for k in range(9):
            own = jnp.where(same, product[:, k * 128 : (k + 1) * 128], 0.0)
            taps.append(jnp.sum(own.reshape(128 // 8, 8, 128), axis=0))
        halves.append(jnp.concatenate(taps, axis=0))
    taps = [jnp.concatenate(halves, axis=1)]
    group = jnp.concatenate(taps + [jnp.zeros((CH - 72, CH), F32)], axis=0).astype(BF16)
    packed_ref[3 * CH :] = group[: packed_ref.shape[0] - 3 * CH]


def near_total_kernel(parts_ref, total_ref):
    total = jnp.sum(parts_ref[...].astype(F32), axis=0)
    spare = total_ref.shape[0] * total_ref.shape[1] - total.shape[0]
    if spare:
        total = jnp.concatenate([total, jnp.zeros((spare, CH), F32)], axis=0)
    total_ref[...] = total.reshape(total_ref.shape).astype(BF16)


def total_kernel(parts_ref, total_ref):
    total = jnp.sum(parts_ref[...].astype(F32), axis=0).astype(BF16)
    total_ref[...] = jnp.broadcast_to(total[None], total_ref.shape)


def repeat_kernel(part_ref, parts_ref):
    part = part_ref[...].reshape(part_ref.shape[0] * part_ref.shape[1], CH)
    part = part[: parts_ref.shape[1]]
    parts_ref[...] = jnp.broadcast_to(part[None], parts_ref.shape)


def unpack_kernel(packed_ref, reduce_ref, group_ref, expand_ref):
    packed = packed_ref[...].astype(F32)
    reduce_ref[...] = packed[:CH]
    expand_ref[:, :CH] = packed[CH : 2 * CH]
    expand_ref[:, CH:] = packed[2 * CH : 3 * CH]
    group_ref[...] = packed[3 * CH : 3 * CH + 72]


def body(
    sizes, activations, tissue, neighbours, w_reduce, w_group, norm_gain, norm_bias, w_expand,
    cotangent,
):
    space, near, far, first, second = sizes
    odd = (lax.axis_index(SPACE) % 2).astype(jnp.int32).reshape(1)
    rim = shape((2 * WIDE, CH), BF16)
    flat = shape((ROWS, CH), BF16)
    full = shape((ROWS, CH), F32)

    def rows_passed(top, bottom):
        up = lax.ppermute(bottom, SPACE, [(i, i + 2) for i in range(space - 2)])
        down = lax.ppermute(top, SPACE, [(i + 2, i) for i in range(space - 2)])
        return up, down

    def column_passed(column):
        return lax.ppermute(column, SPACE, [(i, i ^ 1) for i in range(space)])

    pixels = activations[0]
    beside = column_passed(jnp.stack([pixels[1, :, SIDE - 1], pixels[0, :, 0]]))
    values, top, bottom, side = call(
        reduce_kernel,
        (flat, rim, rim, shape((WIDE, CH), BF16)),
        [SMEM] + [VMEM] * 3,
        [pltpu.VMEM((2, SIDE, WIDE, CH), BF16)],
    )(odd, activations, beside, w_reduce)
    scale, mask, dense, out_grad, hidden_grad = call(
        prepare_kernel,
        (
            shape((2, CH), F32),
            shape((ROWS, 128), F32),
            shape((9, CH, CH), BF16),
            shape((ROWS, OUT), BF16),
            full,
        ),
        [VMEM] * 6,
        [pltpu.VMEM((2, SIDE, WIDE, OUT), BF16)],
    )(
        tissue, w_group, cotangent, w_expand, norm_gain.reshape(1, CH), norm_bias.reshape(1, CH)
    )
    up, down = rows_passed(top, bottom)

    width = 2 * CH + 128
    rim = shape((2 * WIDE, width), F32)
    joint, padded, sums = call(
        conv_kernel,
        (
            shape((ROWS, width), F32),
            shape((2, EXT, CH), BF16),
            shape((near, 1, width), F32),
        ),
        [SMEM] + [VMEM] * 7,
    )(neighbours, values, up, down, side, dense, mask, hidden_grad)
    parts = lax.all_to_all(sums, NEAR, 0, 0)
    sums, top, bottom = call(
        between_rows_kernel, (shape((far, 1, width), F32), rim, rim), [VMEM] * 2
    )(parts, joint)
    up, down = rows_passed(top, bottom)
    parts = lax.all_to_all(sums, FAR, 0, 0)

    expand_grad, sums = call(
        head_kernel,
        (shape((2 * CH, CH), BF16), shape((near, 1, 2 * CH), F32)),
        [VMEM] * 4,
    )(parts, joint, scale, out_grad)
    totals = lax.all_to_all(sums, NEAR, 0, 0)
    sums, column = call(
        between_column_kernel,
        (shape((far, 1, 2 * CH), F32), shape((WIDE, width), F32)),
        [SMEM] + [VMEM] * 4,
    )(odd, totals, joint, up, down)
    side = column_passed(column)
    totals = lax.all_to_all(sums, FAR, 0, 0)

    rows = pl.cdiv(3 * CH + 72, first * 16) * 16
    share = pl.cdiv(rows, second)
    input_grad, packed, gain_grad, bias_grad = call(
        back_kernel,
        (
            shape((SIDE, SIDE, 2, CH), BF16),
            shape((first * rows, CH), BF16),
            shape((1, CH), F32),
            shape((1, CH), F32),
        ),
        [SMEM] + [VMEM] * 12,
        [pltpu.VMEM((2, SIDE, WIDE, CH), BF16), pltpu.VMEM((9, CH, CH), BF16)],
    )(
        neighbours, parts, totals, joint, scale, up, down, side, w_group, padded,
        activations, w_reduce, expand_grad,
    )
    parts = lax.all_to_all(packed.reshape(first, rows, CH), FIRST, 0, 0)
    total = call(near_total_kernel, shape((second, share, CH), BF16), [VMEM])(parts)
    parts = lax.all_to_all(total, SECOND, 0, 0)
    total = call(total_kernel, shape((second, share, CH), BF16), [VMEM])(parts)
    part = lax.all_to_all(total, SECOND, 0, 0)
    parts = call(repeat_kernel, shape((first, rows, CH), BF16), [VMEM])(part)
    gathered = lax.all_to_all(parts, FIRST, 0, 0)
    reduce_grad, group_grad, expand_grad = call(
        unpack_kernel,
        (shape((CH, CH), F32), shape((72, CH), F32), shape((CH, OUT), F32)),
        [VMEM],
    )(gathered.reshape(packed.shape))
    return (
        input_grad[None].transpose(0, 3, 1, 2, 4),
        reduce_grad,
        group_grad.reshape(3, 3, 8, CH),
        gain_grad.reshape(CH),
        bias_grad.reshape(CH),
        expand_grad,
    )


def solution(mesh):
    dp, space = mesh.shape["dp"], mesh.shape["space"]
    zh = max(dp // 4, 1)
    zl = max(space // 16, 1)
    dims = (zh, dp // zh, zl, space // zl // 2, 2)
    cut = Mesh(mesh.devices.reshape(dims), DP + SPACE)

    def count(axes):
        return math.prod(cut.shape[axis] for axis in axes)

    sizes = tuple(count(axes) for axes in (SPACE, NEAR, FAR, FIRST, SECOND))
    return jax.shard_map(
        functools.partial(body, sizes),
        mesh=cut,
        in_specs=(
            P(DP, SPACE, None, None, None),
            P(DP, SPACE, None, None),
            P(DP, SPACE, None),
            P(),
            P(),
            P(),
            P(),
            P(),
            P(DP, SPACE, None, None, None),
        ),
        out_specs=(P(DP, SPACE, None, None, None), P(), P(), P(), P(), P()),
        check_vma=False,
    )
```
